32 devices in a mesh: pole: 2 (over y), prow: 1, pcol: 16 (over z, x, core).
Axes of the slice: x: 2, y: 2, z: 4, core: 2. Of those that a mesh axis runs over, the one named last changes fastest.
Arguments:
- anc_inverse: float32 [12288, 6144], P(('pole', 'prow'), 'pcol'), parts along dimension 0, may hold values from -8 to 8
- anc_factor: float32 [12288, 768], P(('pole', 'pcol')), parts along dimension 0, may hold values from -0.078125 to 0.078125
- win_factor: float32 [1536, 768], P('pole'), parts along dimension 0, may hold values from -0.375 to 0.375
- pivot_inverse: float32 [6, 256, 256], P('pole'), parts along dimension 0, may hold values from -6 to 6
- structure: int32 [3, 24], replicated, may hold values 0 or 1
Outputs:
- anc_columns: float32 [12288, 768], P(('pole', 'prow', 'pcol')), parts along dimension 0
- win_inverse: float32 [1536, 768], P('pole'), parts along dimension 0
The draws below stay inside these ranges and needn't reach their ends.
There are 2 independent parts, one for each index of `pole`. The reference program is written for one: setup_inputs(seed, part) draws one part's arguments, and reference() takes and returns one part's arrays. A program takes and returns all parts, laid end to end along the dimension named above; an argument that names none is the same for every part. Nothing has to cross between parts.
All inputs are finite; a program needn't handle non-finite values.
Results may differ from the reference program's by a relative error of at most 0.0001.
Values sent between devices are 32-bit elements; how exact they have to be, the bound alone decides.
No kernel may reach another device: no remote copies, remote signals or barrier semaphores. Data moves between devices by JAX's collectives and lax.ppermute only.
A program may use at most 128 MiB of HBM per device.

```python
import jax
import jax.numpy as jnp
from jax import lax

W = 256
STEPS = 3
NA = 6144
NAB = 24
SW = 768


def draw_anc_inverse(key, part):
    entry_key = jax.random.fold_in(jax.random.fold_in(key, 11), 0)
    entries = jnp.clip(jax.random.normal(entry_key, (NA, NA), jnp.float32), -5.0, 5.0)
    return (entries + entries.T) * 0.7071


def plant(values, key, low, high):
    index_at = [jax.random.randint(jax.random.fold_in(key, axis), (), 0, length) for axis, length in enumerate(values.shape)]
    widest = values.shape.index(max(values.shape))
    next_to = index_at[:widest] + [(index_at[widest] + 1) % values.shape[widest]] + index_at[widest + 1:]
    return values.at[tuple(index_at)].set(low).at[tuple(next_to)].set(high)


def steps_of(stream_key, dims, cuts, least, high):
    gain = 1.0
    for axis_at, shards_of in cuts:
        heights = jax.random.uniform(jax.random.fold_in(jax.random.fold_in(stream_key, 6), axis_at), (shards_of,), jnp.float32, least / len(cuts), high / len(cuts))
        gain = gain * jnp.repeat(jnp.exp(heights), dims[axis_at] // shards_of).reshape((-1,) + (1,) * (len(dims) - 1 - axis_at))
    return gain


def scatter_about(rng, shape, deviation, reach, cuts=(), kind=jnp.bfloat16):
    array = deviation * jax.random.normal(rng, shape, jnp.float32)
    if cuts:
        array = array * steps_of(rng, shape, cuts, -0.22, 0.18)
    return jnp.clip(array, -reach, reach).astype(kind)


def setup_inputs(seed: int = 0, part: int = 0) -> dict:
    arg_keys = jax.random.split(jax.random.key(seed), 6)
    part_keys = jax.random.split(jax.random.fold_in(arg_keys[5], part), 6)
    anc_inverse = draw_anc_inverse(jax.random.fold_in(jax.random.fold_in(arg_keys[5], part), 71), part)
    anc_factor = scatter_about(part_keys[1], (NA, SW), NA ** -0.5, 0.078125, ((0, 16),), jnp.float32)
    win_factor = scatter_about(part_keys[2], (SW, SW), W ** -0.5, 0.375, (), jnp.float32)
    pivot_inverse = scatter_about(part_keys[3], (STEPS, W, W), 1.0, 6.0, (), jnp.float32)
    structure = plant((jax.random.randint(arg_keys[4], (STEPS, NAB), 0, 4) < 3).astype(jnp.int32), jax.random.fold_in(arg_keys[4], 1), 0, 1)
    return dict(anc_inverse=anc_inverse, anc_factor=anc_factor, win_factor=win_factor, pivot_inverse=pivot_inverse, structure=structure)


precise = lax.Precision.HIGHEST


def product(left, right):
    return jnp.dot(left, right, precision=precise, preferred_element_type=jnp.float32)


def reference(anc_inverse, anc_factor, win_factor, pivot_inverse, structure):
    row_block = (jnp.arange(NA) // W).astype(jnp.int32)
    kept_rows = jnp.take(structure, row_block, axis=1).astype(jnp.float32).T
    column_store = {}
    window_blocks = {}
    for k in range(STEPS - 1, -1, -1):
        first_col = k * W
        factor_now = anc_factor[:, first_col:first_col + W] * kept_rows[:, k:k + 1]
        product_term = product(anc_inverse, factor_now)
        finished = list(range(k + 1, STEPS))
        if finished:
            stacked = jnp.concatenate([column_store[j] for j in finished], axis=1)
            column_now = -(product_term + product(stacked, win_factor[first_col + W:, first_col:first_col + W]))
        else:
            column_now = -product_term
        for j in finished:
            running = product(column_store[j].T, factor_now)
            for i in finished:
                running = running + product(window_blocks[(j, i)], win_factor[i * W:(i + 1) * W, first_col:first_col + W])
            window_blocks[(j, k)] = -running
            window_blocks[(k, j)] = -running.T
        pivot_block = pivot_inverse[k] - product(factor_now.T, column_now)
        for j in finished:
            pivot_block = pivot_block - product(win_factor[j * W:(j + 1) * W, first_col:first_col + W].T, window_blocks[(j, k)])
        window_blocks[(k, k)] = pivot_block
        column_store[k] = column_now
    anc_columns = jnp.concatenate([column_store[k] for k in range(STEPS)], axis=1)
    win_inverse = jnp.concatenate([jnp.concatenate([window_blocks[(i, k)] for k in range(STEPS)], axis=1) for i in range(STEPS)], axis=0)
    return (anc_columns, win_inverse)
```

```python
import functools
import math

import jax
import jax.numpy as jnp
from jax import lax
from jax.experimental import pallas as pl
from jax.experimental.pallas import tpu as pltpu
from jax.sharding import PartitionSpec as P

precise = lax.Precision.HIGHEST


def product(left, right):
    return jnp.dot(left, right, precision=precise, preferred_element_type=jnp.float32)


def on_device(anc_inverse, anc_factor, win_factor, pivot_inverse, structure):
    row_count = lax.axis_size("prow")
    col_count = lax.axis_size("pcol")
    row_index = lax.axis_index("prow")
    col_index = lax.axis_index("pcol")
    block_rows = anc_inverse.shape[0]
    block_cols = anc_inverse.shape[1]
    steps_total = pivot_inverse.shape[0]
    width = pivot_inverse.shape[1]
    all_cols = anc_factor.shape[1]
    block_count = structure.shape[1]
    ratio_cols = col_count // row_count
    share_rows = block_rows // col_count
    structure_cols = structure.T.astype(jnp.float32)
    global_rows = col_index * block_cols + lax.iota(jnp.int32, block_cols)
    onehot_rows = (
        (global_rows // width)[:, None] == lax.iota(jnp.int32, block_count)[None, :]
    ).astype(jnp.float32)
    kept_rows = product(onehot_rows, structure_cols)
    share_offset = col_index * share_rows
    share_global = (row_index * col_count + col_index) * share_rows + lax.iota(
        jnp.int32, share_rows
    )
    onehot_share = (
        (share_global // width)[:, None] == lax.iota(jnp.int32, block_count)[None, :]
    ).astype(jnp.float32)
    kept_share = product(onehot_share, structure_cols)
    slot_ids = lax.iota(jnp.int32, col_count)
    source_flag = (slot_ids // row_count == col_index - row_index * ratio_cols).astype(jnp.float32)
    pieces = jnp.tile(anc_factor.reshape(row_count, share_rows, all_cols), (ratio_cols, 1, 1))
    outgoing = pieces * source_flag[:, None, None]
    incoming = lax.all_to_all(outgoing, "pcol", split_axis=0, concat_axis=0, tiled=True)
    factor_share = jnp.sum(incoming, axis=0)
    column_store = {}
    share_store = {}
    window_blocks = {}
    for k in range(steps_total - 1, -1, -1):
        first_col = k * width
        factor_now = anc_factor[:, first_col : first_col + width] * kept_rows[:, k : k + 1]
        share_factor = factor_share[:, first_col : first_col + width] * kept_share[:, k : k + 1]
        finished = list(range(k + 1, steps_total))
        if finished:
            stacked = jnp.concatenate([column_store[j] for j in finished], axis=1)
            factor_win = win_factor[first_col + width :, first_col : first_col + width]

        def term_rows(start, count, factor_now=factor_now):
            return product(anc_inverse, factor_now)

        share_image = lax.psum_scatter(
            term_rows(jnp.int32(0), share_rows * lax.axis_size("pcol")),
            "pcol",
            scatter_dimension=0,
            tiled=True,
        )
        if finished:
            share_image = share_image + product(
                lax.dynamic_slice_in_dim(stacked, share_offset, share_rows, 0), factor_win
            )
        share_column = -share_image
        column_now = lax.all_gather(share_column, "pcol", axis=0, tiled=True)
        crossings = [product(share_store[j].T, share_factor) for j in finished]
        pivot_part = product(share_factor.T, share_column)
        cross_sums = []
        if finished:
            cross_total = lax.psum(jnp.stack(crossings), ("prow", "pcol"))
            cross_sums = [cross_total[position] for position in range(len(finished))]
        pivot_sum = lax.psum(pivot_part, ("prow", "pcol"))
        for position, j in enumerate(finished):
            running = cross_sums[position]
            for i in finished:
                running = running + product(
                    window_blocks[j, i],
                    win_factor[i * width : (i + 1) * width, first_col : first_col + width],
                )
            window_blocks[j, k] = -running
            window_blocks[k, j] = -running.T
        pivot_block = pivot_inverse[k] - pivot_sum
        for j in finished:
            pivot_block = pivot_block - product(
                win_factor[j * width : (j + 1) * width, first_col : first_col + width].T,
                window_blocks[j, k],
            )
        window_blocks[k, k] = pivot_block
        column_store[k] = column_now
        share_store[k] = share_column
    anc_columns = jnp.concatenate([share_store[k] for k in range(steps_total)], axis=1)
    win_inverse = jnp.concatenate(
        [
            jnp.concatenate([window_blocks[i, k] for k in range(steps_total)], axis=1)
            for i in range(steps_total)
        ],
        axis=0,
    )
    return (anc_columns, win_inverse)


vmem_bytes = 60 * 1024 * 1024
tile = 128
little = pl.CostEstimate(flops=1, bytes_accessed=1, transcendentals=0)


def halves_of(value):
    high = value.astype(jnp.bfloat16)
    return high, (value - high.astype(jnp.float32)).astype(jnp.bfloat16)


def product_of(left, right, turned=False):
    dims = ((0,), (0,)) if turned else ((1,), (0,))

    def dot(a, b):
        return lax.dot_general(a, b, (dims, ((), ())), preferred_element_type=jnp.float32)

    return dot(left[0], right[0]) + dot(left[0], right[1]) + dot(left[1], right[0])


def times(left, right, turned=False):
    return product_of(halves_of(left), halves_of(right), turned)


def chip_at(place, levels):
    return jnp.where(place < levels, 2 * place, 2 * (2 * levels - 1 - place) + 1)


def ring_place(index, levels):
    z = index // 4
    return jnp.where((index // 2) % 2 == 0, z, 2 * levels - 1 - z)


def source_device(step, index, levels):
    away = jnp.where(step % 2 == 1, -((step + 1) // 2), step // 2)
    spot = lax.rem(ring_place(index, levels) + away + 2 * levels, 2 * levels)
    return 2 * chip_at(spot, levels) + index % 2


def head_kernel(width, cuts, index_ref, structure_ref, factor_ref, masked_ref, *turned_refs):
    rows, all_cols = factor_ref.shape
    share = math.gcd(rows, width)
    for t in range(rows // share):
        block = (index_ref[0] * rows + t * share) // width
        at = slice(t * share, (t + 1) * share)
        for k in range(all_cols // width):
            kept = structure_ref[k, block].astype(jnp.float32)
            cols = slice(k * width, (k + 1) * width)
            masked_ref[at, cols] = factor_ref[at, cols] * kept
    for (first, last), ref in zip(cuts, turned_refs):
        ref[...] = masked_ref[:, first:last].T


def head(index, structure, anc_factor, width, cuts):
    rows, all_cols = anc_factor.shape
    smem = pl.BlockSpec(memory_space=pltpu.SMEM)
    vmem = pl.BlockSpec(memory_space=pltpu.VMEM)
    return pl.pallas_call(
        functools.partial(head_kernel, width, cuts),
        in_specs=[smem, smem, vmem],
        out_specs=[vmem] * (1 + len(cuts)),
        out_shape=[jax.ShapeDtypeStruct((rows, all_cols), jnp.float32)]
        + [jax.ShapeDtypeStruct((last - first, rows), jnp.float32) for first, last in cuts],
        compiler_params=pltpu.CompilerParams(vmem_limit_bytes=vmem_bytes),
        cost_estimate=little,
    )(index, structure, anc_factor)


def multiply_kernel(layout, has_start, rows_at, index_ref, own_ref, twin_ref, *refs):
    refs = list(refs)
    piece_count = sum(len(block) for block in layout)
    pieces = [refs.pop(0) for _ in range(piece_count)]
    starts = [refs.pop(0) for _ in range(2)] if has_start else None
    factors = [refs.pop(0) for _ in range(2)] if rows_at else None
    outs = [refs.pop(0) for _ in range(2)]
    inner_ref = refs.pop(0) if rows_at else None
    held = refs.pop(0)
    step = pl.program_id(0)
    at = 0
    for b, block in enumerate(layout):
        chosen = pieces[at : at + len(block)]
        at += len(block)

        @pl.when(step == b)
        def _(chosen=chosen, block=block):
            for ref, (top, height) in zip(chosen, block):
                held[top : top + height, :] = ref[...]

    @pl.when(step == 0)
    def _():
        for i in range(2):
            outs[i][...] = starts[i][...] if has_start else jnp.zeros_like(outs[i])

    rows = halves_of(held[...])
    for ref, out in ((own_ref, outs[0]), (twin_ref, outs[1])):
        out[...] += product_of(rows, halves_of(ref[...]))
    if rows_at:

        @pl.when(step == len(layout) - 1)
        def _():
            images = [halves_of(out[...]) for out in outs]
            sides = [halves_of(ref[...]) for ref in factors]
            spot = 0
            for top, first in rows_at:
                value = 0.0
                for image, side in zip(images, sides):
                    value = value + product_of(
                        tuple(half[top : top + tile] for half in image),
                        tuple(half[:, : first + tile] for half in side),
                    )
                for i in range(first // tile + 1):
                    inner_ref[spot * tile : (spot + 1) * tile, :] = value[
                        :, i * tile : (i + 1) * tile
                    ]
                    spot += 1


def multiply(index, inverse, twin, first, blocks, start=None, rows_at=(), factors=()):
    rows = inverse.shape[1]
    levels = inverse.shape[0] // rows // 4
    layout, flat = [], []
    for block in blocks:
        top, places = 0, []
        for piece in block:
            places.append((top, piece.shape[0]))
            top += piece.shape[0]
            flat.append(piece)
        layout.append(tuple(places))
    height = top

    def whole(shape):
        return pl.BlockSpec(shape, lambda i, at: (0, 0))

    def source(i, at):
        return source_device(i + first, at[0], levels), 0

    image = jax.ShapeDtypeStruct((height, rows), jnp.float32)
    out_shape = [image, image]
    if rows_at:
        count = sum(first // tile + 1 for _, first in rows_at)
        out_shape.append(jax.ShapeDtypeStruct((count * tile, tile), jnp.float32))
    operands = flat + list(start or ()) + list(factors)
    return pl.pallas_call(
        functools.partial(multiply_kernel, tuple(layout), start is not None, rows_at),
        grid_spec=pltpu.PrefetchScalarGridSpec(
            num_scalar_prefetch=1,
            grid=(len(blocks),),
            in_specs=[pl.BlockSpec((rows, rows), source), pl.BlockSpec((rows, rows), source)]
            + [whole(v.shape) for v in operands],
            out_specs=[whole(v.shape) for v in out_shape],
            scratch_shapes=[pltpu.VMEM((height, rows), jnp.float32)],
        ),
        out_shape=out_shape,
        compiler_params=pltpu.CompilerParams(vmem_limit_bytes=vmem_bytes),
        cost_estimate=little,
    )(index, inverse, twin, *operands)


def columns_kernel(width, steps, tops, *refs):
    images, adds = refs[: len(tops)], refs[len(tops) : 2 * len(tops)]
    factor_ref, out_ref, image = refs[2 * len(tops) :]
    for top, ref, add_ref in zip(tops, images, adds):
        image[top : top + ref.shape[0], :] = ref[...] + add_ref[...]
    solved = {}
    for k in range(steps - 1, -1, -1):
        value = image[k * width : (k + 1) * width, :]
        for j in range(k + 1, steps):
            side = factor_ref[j * width : (j + 1) * width, k * width : (k + 1) * width]
            value = value + times(side, solved[j], True)
        solved[k] = -value
        out_ref[:, k * width : (k + 1) * width] = solved[k].T


def solve_columns(width, steps, tops, images, adds, win_factor):
    rows = images[0].shape[1]
    return pl.pallas_call(
        functools.partial(columns_kernel, width, steps, tops),
        out_shape=jax.ShapeDtypeStruct((rows, steps * width), jnp.float32),
        scratch_shapes=[pltpu.VMEM((steps * width, rows), jnp.float32)],
        compiler_params=pltpu.CompilerParams(vmem_limit_bytes=vmem_bytes),
        cost_estimate=little,
    )(*images, *adds, win_factor)


def fill_inner(inner, top, one, two, first_half):
    whole = jnp.concatenate(
        [jnp.where(first_half, one, two), jnp.where(first_half, two, one)], axis=0
    )
    spot, row = 0, top
    while spot * tile < whole.shape[0]:
        for i in range(row // tile + 1):
            block = whole[spot * tile : (spot + 1) * tile]
            spot += 1
            inner[row : row + tile, i * tile : (i + 1) * tile] = block
            if i * tile < row:
                inner[i * tile : (i + 1) * tile, row : row + tile] = block.T
        row += tile


def add_kernel(core_ref, mine_ref, other_ref, base_ref, out_ref, inner):
    fill_inner(inner, 0, mine_ref[...], other_ref[...], core_ref[0] % 2 == 0)
    out_ref[...] = base_ref[...] + inner[...]


def add_last(index, mine, other, base, width):
    block = pl.BlockSpec((width, width), lambda i: (0, 0))
    part = pl.BlockSpec(mine.shape, lambda i: (0, 0))
    return pl.pallas_call(
        add_kernel,
        grid=(1,),
        in_specs=[pl.BlockSpec(memory_space=pltpu.SMEM), part, part, block],
        out_specs=block,
        out_shape=jax.ShapeDtypeStruct(base.shape, jnp.float32),
        input_output_aliases={3: 0},
        scratch_shapes=[pltpu.VMEM((width, width), jnp.float32)],
        compiler_params=pltpu.CompilerParams(vmem_limit_bytes=vmem_bytes),
        cost_estimate=little,
    )(index, mine, other, base)


def window_kernel(width, steps, tops, core_ref, *refs):
    mine, other = refs[: len(tops)], refs[len(tops) : 2 * len(tops)]
    factor_ref, pivot_ref, out_ref, inner = refs[2 * len(tops) :]
    low = min(tops)
    if low:
        inner[:low, :low] = jnp.zeros((low, low), jnp.float32)
    for top, mine_ref, other_ref in zip(tops, mine, other):
        fill_inner(inner, top, mine_ref[...], other_ref[...], core_ref[0] % 2 == 0)

    def at(k):
        return slice(k * width, (k + 1) * width)

    cross = {}
    for k in range(steps - 1, -1, -1):
        later = range(k + 1, steps)
        for i in range(k + 1):
            value = inner[at(k), at(i)]
            for j in later:
                value = value + times(factor_ref[at(j), at(k)], cross[j, i], True)
            cross[k, i] = -value
        for j in later:
            value = cross[j, k]
            for i in later:
                value = value + times(out_ref[at(j), at(i)], factor_ref[at(i), at(k)])
            out_ref[at(j), at(k)] = -value
            out_ref[at(k), at(j)] = -value.T
        value = pivot_ref[k] - cross[k, k].T
        for j in later:
            value = value - times(factor_ref[at(j), at(k)], out_ref[at(j), at(k)], True)
        out_ref[at(k), at(k)] = value


def window_blocks_of(width, steps, tops, index, mine, other, win_factor, pivot_inverse):
    order = steps * width
    vmem = pl.BlockSpec(memory_space=pltpu.VMEM)
    count = 2 * len(tops) + 2
    return pl.pallas_call(
        functools.partial(window_kernel, width, steps, tops),
        in_specs=[pl.BlockSpec(memory_space=pltpu.SMEM)] + [vmem] * count,
        out_specs=vmem,
        out_shape=jax.ShapeDtypeStruct((order, order), jnp.float32),
        scratch_shapes=[pltpu.VMEM((order, order), jnp.float32)],
        compiler_params=pltpu.CompilerParams(vmem_limit_bytes=vmem_bytes),
        cost_estimate=little,
    )(index, *mine, *other, win_factor, pivot_inverse)


def fast(anc_inverse, anc_factor, win_factor, pivot_inverse, structure):
    n = lax.axis_size("pcol")
    index = lax.axis_index("pcol")
    levels = n // 4
    chips = n // 2
    half_way = chips // 2
    core = index % 2
    x = (index // 2) % 2
    z = index // 4
    rows = anc_inverse.shape[1]
    steps_total, width = pivot_inverse.shape[:2]
    all_cols = anc_factor.shape[1]
    order = [2 * s if s < levels else 2 * (chips - 1 - s) + 1 for s in range(chips)]
    forward = [
        (2 * order[s] + c, 2 * order[(s + 1) % chips] + c) for s in range(chips) for c in range(2)
    ]
    backward = [(to, start) for start, to in forward]

    def flip(bits):
        return [(p, p ^ bits) for p in range(n)]

    def send(value, pairs):
        return lax.ppermute(value, "pcol", pairs)

    def pick(value, at):
        return lax.dynamic_index_in_dim(value, at, 0, keepdims=False)

    def swap_halves(value, bit):
        halves = value.reshape((2, value.shape[0] // 2) + value.shape[1:])
        return pick(halves, bit), pick(halves, 1 - bit)

    def join(bit, mine, other):
        return jnp.concatenate(
            [jnp.where(bit == 0, mine, other), jnp.where(bit == 0, other, mine)], axis=0
        )

    def sum_small(value):
        mine, other = swap_halves(value, core)
        got = yield [send(other, flip(1))]
        mine = mine + got[0]
        got = yield [send(mine, flip(2))]
        mine = mine + got[0]
        got = yield [send(mine, flip(4 * d)) for d in range(1, levels)]
        for value in got:
            mine = mine + value
        got = yield [send(mine, flip(1))]
        yield mine, got[0]

    def sum_large(value):
        mine, other = swap_halves(value, core)
        got = yield [send(other, flip(1))]
        mine, other = swap_halves(mine + got[0], x)
        got = yield [send(other, flip(2))]
        mine = mine + got[0]
        parts = mine.reshape((levels, mine.shape[0] // levels) + mine.shape[1:])
        got = yield [send(pick(parts, z ^ d), flip(4 * d)) for d in range(1, levels)]
        total = pick(parts, z)
        for value in got:
            total = total + value
        got = yield [send(total, flip(4 * d)) for d in range(1, levels)]
        pieces = [total] + got
        bit = 1
        while bit < levels:
            pieces = [
                join((z // bit) % 2, pieces[i], pieces[i + 1]) for i in range(0, len(pieces), 2)
            ]
            bit *= 2
        mine = pieces[0]
        got = yield [send(mine, flip(2))]
        mine = join(x, mine, got[0])
        got = yield [send(mine, flip(1))]
        yield mine, got[0]

    def ends(up, down):
        middle = up.shape[0] // 2
        return [send(up[:middle], forward), send(down[middle:], backward)]

    at = index.astype(jnp.int32).reshape(1)
    plan = (((width, 2 * width), (2 * width, all_cols)), ((0, width),))
    cuts = tuple(cut for streams in plan for cut in streams)
    factor, *turned = head(at, structure, anc_factor, width, cuts)
    twin = send(anc_inverse, flip(1))
    factor_twin = send(factor, flip(1))
    factors = (factor, factor_twin)

    def ring(pieces):
        ups = downs = list(pieces)
        yield ups, ups
        for s in range(1, half_way):
            ups = [send(v, forward) for v in ups]
            downs = [send(v, backward) for v in downs]
            ups, downs = yield ups, downs
        if len(ups) == 2:
            yield [send(ups[0], forward), send(downs[1], backward)]
        else:
            yield ends(ups[0], downs[0])

    def strips(streams):
        first, last = streams[0][0], streams[-1][1]
        return tuple((i - first, i) for i in range(first, last, tile))

    def product(start, blocks, total=None, rows_at=()):
        return multiply(
            at, anc_inverse, twin, start, blocks, total, rows_at, factors if rows_at else ()
        )

    hold = lax.optimization_barrier
    ring_a = ring(turned[: len(plan[0])])
    pieces_b = turned[len(plan[0]) :]
    ups, _ = next(ring_a)
    a = [ups]
    ups, downs = next(ring_a)
    for s in range(2, half_way):
        a += [ups, downs]
        ups, downs = ring_a.send((ups, downs))
    near = product(0, a)
    (ups, downs), near = hold(((ups, downs), near))
    pieces_b, downs = hold((pieces_b, downs))
    far = ring_a.send((ups, downs))
    ring_b = ring(pieces_b)
    b = [next(ring_b)[0]]
    ups_b, downs_b = next(ring_b)
    mid = product(5, [ups, downs], near)
    mine_a, theirs_a, local = product(7, [far], mid, strips(plan[0]))
    (ups_b, downs_b), local = hold(((ups_b, downs_b), local))
    sum_a = sum_large(local)
    got = next(sum_a)
    b += [ups_b, downs_b]
    ups_b, downs_b = ring_b.send((ups_b, downs_b))
    (ups_b, downs_b), got = hold(((ups_b, downs_b), got))
    got = sum_a.send(got)
    adds_a = send(theirs_a, flip(1))
    b += [ups_b, downs_b]
    near = product(0, b)
    ups_b, downs_b = ring_b.send((ups_b, downs_b))
    (ups_b, downs_b), got, near = hold(((ups_b, downs_b), got, near))
    got = sum_a.send(got)
    far = ring_b.send((ups_b, downs_b))
    mid = product(5, [ups_b, downs_b], near)
    got = sum_a.send(got)
    mine_b, theirs_b, local = product(7, [far], mid, strips(plan[1]))
    sum_b = sum_small(local)
    got_b = next(sum_b)
    got_b, got = hold((got_b, got))
    got = sum_a.send(got)
    got_b = sum_b.send(got_b)
    adds_b = send(theirs_b, flip(1))
    got_b, got = hold((got_b, got))
    got = sum_a.send(got)
    got_b = sum_b.send(got_b)
    tops = [plan[0][0][0], plan[1][0][0]]
    images, adds = [mine_a, mine_b], [adds_a, adds_b]
    anc_columns = solve_columns(width, steps_total, tops, images, adds, win_factor)
    got_b, got, anc_columns = hold((got_b, got, anc_columns))
    got_b = sum_b.send(got_b)
    mine, other = sum_a.send(got)
    base = window_blocks_of(
        width, steps_total, tops[:1], at, [mine], [other], win_factor, pivot_inverse
    )
    win_inverse = add_last(at, *sum_b.send(got_b), base, width)
    return (anc_columns, win_inverse)


def solution(mesh):
    in_specs = (
        P(("pole", "prow"), "pcol"),
        P(("pole", "pcol"), None),
        P("pole", None),
        P("pole", None, None),
        P(),
    )
    out_specs = (P(("pole", "prow", "pcol"), None), P("pole", None))
    levels = mesh.shape["pcol"] // 4
    ringed = mesh.shape["prow"] == 1 and mesh.shape["pcol"] % 4 == 0
    ringed = ringed and levels > 1 and levels & (levels - 1) == 0
    return jax.shard_map(
        fast if ringed else on_device, mesh=mesh, in_specs=in_specs, out_specs=out_specs, check_vma=False
    )
```

```python
import functools
import math

import jax
import jax.numpy as jnp
from jax import lax
from jax.experimental import pallas as pl
from jax.experimental.pallas import tpu as pltpu
from jax.sharding import PartitionSpec as P

precise = lax.Precision.HIGHEST


def product(left, right):
    return jnp.dot(left, right, precision=precise, preferred_element_type=jnp.float32)


def on_device(anc_inverse, anc_factor, win_factor, pivot_inverse, structure):
    row_count = lax.axis_size("prow")
    col_count = lax.axis_size("pcol")
    row_index = lax.axis_index("prow")
    col_index = lax.axis_index("pcol")
    block_rows = anc_inverse.shape[0]
    block_cols = anc_inverse.shape[1]
    steps_total = pivot_inverse.shape[0]
    width = pivot_inverse.shape[1]
    all_cols = anc_factor.shape[1]
    block_count = structure.shape[1]
    ratio_cols = col_count // row_count
    share_rows = block_rows // col_count
    structure_cols = structure.T.astype(jnp.float32)
    global_rows = col_index * block_cols + lax.iota(jnp.int32, block_cols)
    onehot_rows = (
        (global_rows // width)[:, None] == lax.iota(jnp.int32, block_count)[None, :]
    ).astype(jnp.float32)
    kept_rows = product(onehot_rows, structure_cols)
    share_offset = col_index * share_rows
    share_global = (row_index * col_count + col_index) * share_rows + lax.iota(
        jnp.int32, share_rows
    )
    onehot_share = (
        (share_global // width)[:, None] == lax.iota(jnp.int32, block_count)[None, :]
    ).astype(jnp.float32)
    kept_share = product(onehot_share, structure_cols)
    slot_ids = lax.iota(jnp.int32, col_count)
    source_flag = (slot_ids // row_count == col_index - row_index * ratio_cols).astype(jnp.float32)
    pieces = jnp.tile(anc_factor.reshape(row_count, share_rows, all_cols), (ratio_cols, 1, 1))
    outgoing = pieces * source_flag[:, None, None]
    incoming = lax.all_to_all(outgoing, "pcol", split_axis=0, concat_axis=0, tiled=True)
    factor_share = jnp.sum(incoming, axis=0)
    column_store = {}
    share_store = {}
    window_blocks = {}
    for k in range(steps_total - 1, -1, -1):
        first_col = k * width
        factor_now = anc_factor[:, first_col : first_col + width] * kept_rows[:, k : k + 1]
        share_factor = factor_share[:, first_col : first_col + width] * kept_share[:, k : k + 1]
        finished = list(range(k + 1, steps_total))
        if finished:
            stacked = jnp.concatenate([column_store[j] for j in finished], axis=1)
            factor_win = win_factor[first_col + width :, first_col : first_col + width]

        def term_rows(start, count, factor_now=factor_now):
            return product(anc_inverse, factor_now)

        share_image = lax.psum_scatter(
            term_rows(jnp.int32(0), share_rows * lax.axis_size("pcol")),
            "pcol",
            scatter_dimension=0,
            tiled=True,
        )
        if finished:
            share_image = share_image + product(
                lax.dynamic_slice_in_dim(stacked, share_offset, share_rows, 0), factor_win
            )
        share_column = -share_image
        column_now = lax.all_gather(share_column, "pcol", axis=0, tiled=True)
        crossings = [product(share_store[j].T, share_factor) for j in finished]
        pivot_part = product(share_factor.T, share_column)
        cross_sums = []
        if finished:
            cross_total = lax.psum(jnp.stack(crossings), ("prow", "pcol"))
            cross_sums = [cross_total[position] for position in range(len(finished))]
        pivot_sum = lax.psum(pivot_part, ("prow", "pcol"))
        for position, j in enumerate(finished):
            running = cross_sums[position]
            for i in finished:
                running = running + product(
                    window_blocks[j, i],
                    win_factor[i * width : (i + 1) * width, first_col : first_col + width],
                )
            window_blocks[j, k] = -running
            window_blocks[k, j] = -running.T
        pivot_block = pivot_inverse[k] - pivot_sum
        for j in finished:
            pivot_block = pivot_block - product(
                win_factor[j * width : (j + 1) * width, first_col : first_col + width].T,
                window_blocks[j, k],
            )
        window_blocks[k, k] = pivot_block
        column_store[k] = column_now
        share_store[k] = share_column
    anc_columns = jnp.concatenate([share_store[k] for k in range(steps_total)], axis=1)
    win_inverse = jnp.concatenate(
        [
            jnp.concatenate([window_blocks[i, k] for k in range(steps_total)], axis=1)
            for i in range(steps_total)
        ],
        axis=0,
    )
    return (anc_columns, win_inverse)


vmem_bytes = 60 * 1024 * 1024
tile = 128
little = pl.CostEstimate(flops=1, bytes_accessed=1, transcendentals=0)


def halves_of(value):
    high = value.astype(jnp.bfloat16)
    return high, (value - high.astype(jnp.float32)).astype(jnp.bfloat16)


def product_of(left, right, turned=False):
    dims = ((0,), (0,)) if turned else ((1,), (0,))

    def dot(a, b):
        return lax.dot_general(a, b, (dims, ((), ())), preferred_element_type=jnp.float32)

    return dot(left[0], right[0]) + dot(left[0], right[1]) + dot(left[1], right[0])


def times(left, right, turned=False):
    return product_of(halves_of(left), halves_of(right), turned)


def chip_at(place, levels):
    return jnp.where(place < levels, 2 * place, 2 * (2 * levels - 1 - place) + 1)


def ring_place(index, levels):
    z = index // 4
    return jnp.where((index // 2) % 2 == 0, z, 2 * levels - 1 - z)


def source_device(step, index, levels):
    away = jnp.where(step % 2 == 1, -((step + 1) // 2), step // 2)
    spot = lax.rem(ring_place(index, levels) + away + 2 * levels, 2 * levels)
    return 2 * chip_at(spot, levels) + index % 2


def head_kernel(width, cuts, index_ref, structure_ref, factor_ref, masked_ref, *turned_refs):
    rows, all_cols = factor_ref.shape
    share = math.gcd(rows, width)
    for t in range(rows // share):
        block = (index_ref[0] * rows + t * share) // width
        at = slice(t * share, (t + 1) * share)
        for k in range(all_cols // width):
            kept = structure_ref[k, block].astype(jnp.float32)
            cols = slice(k * width, (k + 1) * width)
            masked_ref[at, cols] = factor_ref[at, cols] * kept
    for (first, last), ref in zip(cuts, turned_refs):
        ref[...] = masked_ref[:, first:last].T


def head(index, structure, anc_factor, width, cuts):
    rows, all_cols = anc_factor.shape
    smem = pl.BlockSpec(memory_space=pltpu.SMEM)
    vmem = pl.BlockSpec(memory_space=pltpu.VMEM)
    return pl.pallas_call(
        functools.partial(head_kernel, width, cuts),
        in_specs=[smem, smem, vmem],
        out_specs=[vmem] * (1 + len(cuts)),
        out_shape=[jax.ShapeDtypeStruct((rows, all_cols), jnp.float32)]
        + [jax.ShapeDtypeStruct((last - first, rows), jnp.float32) for first, last in cuts],
        compiler_params=pltpu.CompilerParams(vmem_limit_bytes=vmem_bytes),
        cost_estimate=little,
    )(index, structure, anc_factor)


def multiply_kernel(layout, has_start, rows_at, index_ref, *refs):
    refs = list(refs)
    sources = [refs.pop(0) for _ in range(4)]
    piece_count = sum(len(block) for block in layout)
    pieces = [refs.pop(0) for _ in range(piece_count)]
    starts = [refs.pop(0) for _ in range(2)] if has_start else None
    factors = [refs.pop(0) for _ in range(2)] if rows_at else None
    outs = [refs.pop(0) for _ in range(2)]
    inner_ref = refs.pop(0) if rows_at else None
    held = refs.pop(0)
    rows = sources[0].shape[1]
    step = pl.program_id(0)
    at = 0
    for b, block in enumerate(layout):
        chosen = pieces[at : at + len(block)]
        at += len(block)
        left = (b % 2) * rows

        @pl.when(step == b // 2)
        def _(chosen=chosen, block=block, left=left):
            for ref, (top, height) in zip(chosen, block):
                held[top : top + height, left : left + rows] = ref[...]

    @pl.when(step == 0)
    def _():
        for i in range(2):
            outs[i][...] = starts[i][...] if has_start else jnp.zeros_like(outs[i])

    inverse = jnp.concatenate(
        [
            jnp.concatenate([own[...], twin[...]], axis=1)
            for own, twin in (sources[:2], sources[2:])
        ],
        axis=0,
    )
    value = product_of(halves_of(held[...]), halves_of(inverse))
    for i in range(2):
        outs[i][...] += value[:, i * rows : (i + 1) * rows]
    if rows_at:

        @pl.when(step == len(layout) // 2 - 1)
        def _():
            image = halves_of(jnp.concatenate([out[...] for out in outs], axis=1))
            side = halves_of(jnp.concatenate([ref[...] for ref in factors], axis=0))
            spot = 0
            for top, first in rows_at:
                value = product_of(
                    tuple(half[top : top + tile] for half in image),
                    tuple(half[:, : first + tile] for half in side),
                )
                for i in range(first // tile + 1):
                    inner_ref[spot * tile : (spot + 1) * tile, :] = value[
                        :, i * tile : (i + 1) * tile
                    ]
                    spot += 1


def multiply(index, inverse, twin, first, blocks, start=None, rows_at=(), factors=()):
    rows = inverse.shape[1]
    levels = inverse.shape[0] // rows // 4
    layout, flat = [], []
    for block in blocks:
        top, places = 0, []
        for piece in block:
            places.append((top, piece.shape[0]))
            top += piece.shape[0]
            flat.append(piece)
        layout.append(tuple(places))
    height = top

    def whole(shape):
        return pl.BlockSpec(shape, lambda i, at: (0, 0))

    def source(side):
        return pl.BlockSpec(
            (rows, rows), lambda i, at: (source_device(first + 2 * i + side, at[0], levels), 0)
        )

    image = jax.ShapeDtypeStruct((height, rows), jnp.float32)
    out_shape = [image, image]
    if rows_at:
        count = sum(first // tile + 1 for _, first in rows_at)
        out_shape.append(jax.ShapeDtypeStruct((count * tile, tile), jnp.float32))
    operands = flat + list(start or ()) + list(factors)
    return pl.pallas_call(
        functools.partial(multiply_kernel, tuple(layout), start is not None, rows_at),
        grid_spec=pltpu.PrefetchScalarGridSpec(
            num_scalar_prefetch=1,
            grid=(len(blocks) // 2,),
            in_specs=[source(0), source(0), source(1), source(1)]
            + [whole(v.shape) for v in operands],
            out_specs=[whole(v.shape) for v in out_shape],
            scratch_shapes=[pltpu.VMEM((height, 2 * rows), jnp.float32)],
        ),
        out_shape=out_shape,
        compiler_params=pltpu.CompilerParams(vmem_limit_bytes=vmem_bytes),
        cost_estimate=little,
    )(index, inverse, twin, inverse, twin, *operands)


def columns_kernel(width, steps, image_ref, add_ref, factor_ref, out_ref):
    solved = {}
    for k in range(steps - 1, -1, -1):
        if k:
            at = slice((k - 1) * width, k * width)
            value = image_ref[at, :] + add_ref[at, :]
        else:
            value = jnp.zeros((width, image_ref.shape[1]), jnp.float32)
        for j in range(k + 1, steps):
            side = factor_ref[j * width : (j + 1) * width, k * width : (k + 1) * width]
            value = value + times(side, solved[j], True)
        solved[k] = -value
        out_ref[:, k * width : (k + 1) * width] = solved[k].T


def solve_columns(width, steps, image, add, win_factor):
    rows = image.shape[1]
    return pl.pallas_call(
        functools.partial(columns_kernel, width, steps),
        out_shape=jax.ShapeDtypeStruct((rows, steps * width), jnp.float32),
        compiler_params=pltpu.CompilerParams(vmem_limit_bytes=vmem_bytes),
        cost_estimate=little,
    )(image, add, win_factor)


def fill_inner(inner, top, one, two, first_half):
    whole = jnp.concatenate(
        [jnp.where(first_half, one, two), jnp.where(first_half, two, one)], axis=0
    )
    spot, row = 0, top
    while spot * tile < whole.shape[0]:
        for i in range(row // tile + 1):
            block = whole[spot * tile : (spot + 1) * tile]
            spot += 1
            inner[row : row + tile, i * tile : (i + 1) * tile] = block
            if i * tile < row:
                inner[i * tile : (i + 1) * tile, row : row + tile] = block.T
        row += tile


def last_kernel(
    core_ref, mine_ref, other_ref, image_ref, add_ref, columns_ref, base_ref, *refs
):
    columns_out, window_out, inner = refs
    columns_out[...] = columns_ref[...] - (image_ref[...] + add_ref[...]).T
    fill_inner(inner, 0, mine_ref[...], other_ref[...], core_ref[0] % 2 == 0)
    window_out[...] = base_ref[...] + inner[...]


def add_last(index, mine, other, image, add, columns, base):
    width, rows = image.shape
    column_block = pl.BlockSpec((rows, width), lambda i: (0, 0))
    window_block = pl.BlockSpec((width, width), lambda i: (0, 0))
    part = pl.BlockSpec(mine.shape, lambda i: (0, 0))
    whole = pl.BlockSpec(image.shape, lambda i: (0, 0))
    return pl.pallas_call(
        last_kernel,
        grid=(1,),
        in_specs=[pl.BlockSpec(memory_space=pltpu.SMEM), part, part, whole, whole]
        + [column_block, window_block],
        out_specs=[column_block, window_block],
        out_shape=[
            jax.ShapeDtypeStruct(columns.shape, jnp.float32),
            jax.ShapeDtypeStruct(base.shape, jnp.float32),
        ],
        input_output_aliases={5: 0, 6: 1},
        scratch_shapes=[pltpu.VMEM((width, width), jnp.float32)],
        compiler_params=pltpu.CompilerParams(vmem_limit_bytes=vmem_bytes),
        cost_estimate=little,
    )(index, mine, other, image, add, columns, base)


def window_kernel(width, steps, tops, core_ref, *refs):
    mine, other = refs[: len(tops)], refs[len(tops) : 2 * len(tops)]
    factor_ref, pivot_ref, out_ref, inner = refs[2 * len(tops) :]
    low = min(tops)
    if low:
        inner[:low, :low] = jnp.zeros((low, low), jnp.float32)
    for top, mine_ref, other_ref in zip(tops, mine, other):
        fill_inner(inner, top, mine_ref[...], other_ref[...], core_ref[0] % 2 == 0)

    def at(k):
        return slice(k * width, (k + 1) * width)

    cross = {}
    for k in range(steps - 1, -1, -1):
        later = range(k + 1, steps)
        for i in range(k + 1):
            value = inner[at(k), at(i)]
            for j in later:
                value = value + times(factor_ref[at(j), at(k)], cross[j, i], True)
            cross[k, i] = -value
        for j in later:
            value = cross[j, k]
            for i in later:
                value = value + times(out_ref[at(j), at(i)], factor_ref[at(i), at(k)])
            out_ref[at(j), at(k)] = -value
            out_ref[at(k), at(j)] = -value.T
        value = pivot_ref[k] - cross[k, k].T
        for j in later:
            value = value - times(factor_ref[at(j), at(k)], out_ref[at(j), at(k)], True)
        out_ref[at(k), at(k)] = value


def window_blocks_of(width, steps, tops, index, mine, other, win_factor, pivot_inverse):
    order = steps * width
    vmem = pl.BlockSpec(memory_space=pltpu.VMEM)
    count = 2 * len(tops) + 2
    return pl.pallas_call(
        functools.partial(window_kernel, width, steps, tops),
        in_specs=[pl.BlockSpec(memory_space=pltpu.SMEM)] + [vmem] * count,
        out_specs=vmem,
        out_shape=jax.ShapeDtypeStruct((order, order), jnp.float32),
        scratch_shapes=[pltpu.VMEM((order, order), jnp.float32)],
        compiler_params=pltpu.CompilerParams(vmem_limit_bytes=vmem_bytes),
        cost_estimate=little,
    )(index, *mine, *other, win_factor, pivot_inverse)


def fast(anc_inverse, anc_factor, win_factor, pivot_inverse, structure):
    n = lax.axis_size("pcol")
    index = lax.axis_index("pcol")
    levels = n // 4
    chips = n // 2
    half_way = chips // 2
    core = index % 2
    x = (index // 2) % 2
    z = index // 4
    rows = anc_inverse.shape[1]
    steps_total, width = pivot_inverse.shape[:2]
    all_cols = anc_factor.shape[1]
    order = [2 * s if s < levels else 2 * (chips - 1 - s) + 1 for s in range(chips)]
    forward = [
        (2 * order[s] + c, 2 * order[(s + 1) % chips] + c) for s in range(chips) for c in range(2)
    ]
    backward = [(to, start) for start, to in forward]

    def flip(bits):
        return [(p, p ^ bits) for p in range(n)]

    def send(value, pairs):
        return lax.ppermute(value, "pcol", pairs)

    def pick(value, at):
        return lax.dynamic_index_in_dim(value, at, 0, keepdims=False)

    def swap_halves(value, bit):
        halves = value.reshape((2, value.shape[0] // 2) + value.shape[1:])
        return pick(halves, bit), pick(halves, 1 - bit)

    def join(bit, mine, other):
        return jnp.concatenate(
            [jnp.where(bit == 0, mine, other), jnp.where(bit == 0, other, mine)], axis=0
        )

    def sum_small(value):
        mine, other = swap_halves(value, core)
        got = yield [send(other, flip(1))]
        mine = mine + got[0]
        got = yield [send(mine, flip(2))]
        mine = mine + got[0]
        got = yield [send(mine, flip(4 * d)) for d in range(1, levels)]
        for value in got:
            mine = mine + value
        got = yield [send(mine, flip(1))]
        yield mine, got[0]

    def sum_large(value):
        mine, other = swap_halves(value, core)
        got = yield [send(other, flip(1))]
        mine, other = swap_halves(mine + got[0], x)
        got = yield [send(other, flip(2))]
        mine = mine + got[0]
        parts = mine.reshape((levels, mine.shape[0] // levels) + mine.shape[1:])
        got = yield [send(pick(parts, z ^ d), flip(4 * d)) for d in range(1, levels)]
        total = pick(parts, z)
        for value in got:
            total = total + value
        got = yield [send(total, flip(4 * d)) for d in range(1, levels)]
        pieces = [total] + got
        bit = 1
        while bit < levels:
            pieces = [
                join((z // bit) % 2, pieces[i], pieces[i + 1]) for i in range(0, len(pieces), 2)
            ]
            bit *= 2
        mine = pieces[0]
        got = yield [send(mine, flip(2))]
        mine = join(x, mine, got[0])
        got = yield [send(mine, flip(1))]
        yield mine, got[0]

    def ends(up, down):
        middle = up.shape[0] // 2
        return [send(up[:middle], forward), send(down[middle:], backward)]

    at = index.astype(jnp.int32).reshape(1)
    plan = (((width, 2 * width), (2 * width, all_cols)), ((0, width),))
    cuts = tuple(cut for streams in plan for cut in streams)
    factor, *turned = head(at, structure, anc_factor, width, cuts)
    twin = send(anc_inverse, flip(1))
    factor_twin = send(factor, flip(1))
    factors = (factor, factor_twin)

    def ring(pieces):
        ups = downs = list(pieces)
        yield ups, ups
        for s in range(1, half_way):
            ups = [send(v, forward) for v in ups]
            downs = [send(v, backward) for v in downs]
            ups, downs = yield ups, downs
        if len(ups) == 2:
            yield [send(ups[0], forward), send(downs[1], backward)]
        else:
            yield ends(ups[0], downs[0])

    def strips(streams):
        first, last = streams[0][0], streams[-1][1]
        return tuple((i - first, i) for i in range(first, last, tile))

    def product(start, blocks, total=None, rows_at=()):
        return multiply(
            at, anc_inverse, twin, start, blocks, total, rows_at, factors if rows_at else ()
        )

    hold = lax.optimization_barrier
    ring_a = ring(turned[: len(plan[0])])
    pieces_b = turned[len(plan[0]) :]
    a = [next(ring_a)[0]]
    ups_a, downs_a = next(ring_a)
    a += [ups_a, downs_a]
    ups_a, downs_a = ring_a.send((ups_a, downs_a))
    a += [ups_a, downs_a]
    ups_a, downs_a = ring_a.send((ups_a, downs_a))
    near = product(0, a[:4])
    (ups_a, downs_a), near = hold(((ups_a, downs_a), near))
    pieces_b, downs_a = hold((pieces_b, downs_a))
    far = ring_a.send((ups_a, downs_a))
    a += [ups_a, downs_a, far]
    ring_b = ring(pieces_b)
    b = [next(ring_b)[0]]
    ups_b, downs_b = next(ring_b)
    mid = product(4, a[4:6], near)
    mine_a, theirs_a, local = product(6, a[6:], mid, strips(plan[0]))
    (ups_b, downs_b), local = hold(((ups_b, downs_b), local))
    sum_a = sum_large(local)
    got = next(sum_a)
    got = sum_a.send(got)
    b += [ups_b, downs_b]
    ups_b, downs_b = ring_b.send((ups_b, downs_b))
    adds_a = send(theirs_a, flip(1))
    b += [ups_b, downs_b]
    near = product(0, b[:4])
    (ups_b, downs_b), got, near = hold(((ups_b, downs_b), got, near))
    got = sum_a.send(got)
    ups_b, downs_b = ring_b.send((ups_b, downs_b))
    b += [ups_b, downs_b]
    mid = product(4, b[4:6], near)
    columns = solve_columns(width, steps_total, mine_a, adds_a, win_factor)
    got, mid, columns = hold((got, mid, columns))
    got = sum_a.send(got)
    b += [ring_b.send((ups_b, downs_b))]
    mine_b, theirs_b, local = product(6, b[6:], mid, strips(plan[1]))
    adds_b = send(theirs_b, flip(1))
    sum_b = sum_small(local)
    got_b = next(sum_b)
    got = sum_a.send(got)
    got_b, got = hold((got_b, got))
    got_b = sum_b.send(got_b)
    got = sum_a.send(got)
    got_b, got = hold((got_b, got))
    got_b = sum_b.send(got_b)
    mine, other = sum_a.send(got)
    base = window_blocks_of(
        width, steps_total, (width,), at, [mine], [other], win_factor, pivot_inverse
    )
    got_b, base = hold((got_b, base))
    got_b = sum_b.send(got_b)
    anc_columns, win_inverse = add_last(
        at, *sum_b.send(got_b), mine_b, adds_b, columns, base
    )
    return (anc_columns, win_inverse)


def solution(mesh):
    in_specs = (
        P(("pole", "prow"), "pcol"),
        P(("pole", "pcol"), None),
        P("pole", None),
        P("pole", None, None),
        P(),
    )
    out_specs = (P(("pole", "prow", "pcol"), None), P("pole", None))
    levels = mesh.shape["pcol"] // 4
    ringed = mesh.shape["prow"] == 1 and mesh.shape["pcol"] % 4 == 0
    ringed = ringed and levels > 1 and levels & (levels - 1) == 0
    return jax.shard_map(
        fast if ringed else on_device, mesh=mesh, in_specs=in_specs, out_specs=out_specs, check_vma=False
    )
```

```python
import functools
import math

import jax
import jax.numpy as jnp
from jax import lax
from jax.experimental import pallas as pl
from jax.experimental.pallas import tpu as pltpu
from jax.sharding import PartitionSpec as P

precise = lax.Precision.HIGHEST


def product(left, right):
    return jnp.dot(left, right, precision=precise, preferred_element_type=jnp.float32)


def on_device(anc_inverse, anc_factor, win_factor, pivot_inverse, structure):
    row_count = lax.axis_size("prow")
    col_count = lax.axis_size("pcol")
    row_index = lax.axis_index("prow")
    col_index = lax.axis_index("pcol")
    block_rows = anc_inverse.shape[0]
    block_cols = anc_inverse.shape[1]
    steps_total = pivot_inverse.shape[0]
    width = pivot_inverse.shape[1]
    all_cols = anc_factor.shape[1]
    block_count = structure.shape[1]
    ratio_cols = col_count // row_count
    share_rows = block_rows // col_count
    structure_cols = structure.T.astype(jnp.float32)
    global_rows = col_index * block_cols + lax.iota(jnp.int32, block_cols)
    onehot_rows = (
        (global_rows // width)[:, None] == lax.iota(jnp.int32, block_count)[None, :]
    ).astype(jnp.float32)
    kept_rows = product(onehot_rows, structure_cols)
    share_offset = col_index * share_rows
    share_global = (row_index * col_count + col_index) * share_rows + lax.iota(
        jnp.int32, share_rows
    )
    onehot_share = (
        (share_global // width)[:, None] == lax.iota(jnp.int32, block_count)[None, :]
    ).astype(jnp.float32)
    kept_share = product(onehot_share, structure_cols)
    slot_ids = lax.iota(jnp.int32, col_count)
    source_flag = (slot_ids // row_count == col_index - row_index * ratio_cols).astype(jnp.float32)
    pieces = jnp.tile(anc_factor.reshape(row_count, share_rows, all_cols), (ratio_cols, 1, 1))
    outgoing = pieces * source_flag[:, None, None]
    incoming = lax.all_to_all(outgoing, "pcol", split_axis=0, concat_axis=0, tiled=True)
    factor_share = jnp.sum(incoming, axis=0)
    column_store = {}
    share_store = {}
    window_blocks = {}
    for k in range(steps_total - 1, -1, -1):
        first_col = k * width
        factor_now = anc_factor[:, first_col : first_col + width] * kept_rows[:, k : k + 1]
        share_factor = factor_share[:, first_col : first_col + width] * kept_share[:, k : k + 1]
        finished = list(range(k + 1, steps_total))
        if finished:
            stacked = jnp.concatenate([column_store[j] for j in finished], axis=1)
            factor_win = win_factor[first_col + width :, first_col : first_col + width]

        def term_rows(start, count, factor_now=factor_now):
            return product(anc_inverse, factor_now)

        share_image = lax.psum_scatter(
            term_rows(jnp.int32(0), share_rows * lax.axis_size("pcol")),
            "pcol",
            scatter_dimension=0,
            tiled=True,
        )
        if finished:
            share_image = share_image + product(
                lax.dynamic_slice_in_dim(stacked, share_offset, share_rows, 0), factor_win
            )
        share_column = -share_image
        column_now = lax.all_gather(share_column, "pcol", axis=0, tiled=True)
        crossings = [product(share_store[j].T, share_factor) for j in finished]
        pivot_part = product(share_factor.T, share_column)
        cross_sums = []
        if finished:
            cross_total = lax.psum(jnp.stack(crossings), ("prow", "pcol"))
            cross_sums = [cross_total[position] for position in range(len(finished))]
        pivot_sum = lax.psum(pivot_part, ("prow", "pcol"))
        for position, j in enumerate(finished):
            running = cross_sums[position]
            for i in finished:
                running = running + product(
                    window_blocks[j, i],
                    win_factor[i * width : (i + 1) * width, first_col : first_col + width],
                )
            window_blocks[j, k] = -running
            window_blocks[k, j] = -running.T
        pivot_block = pivot_inverse[k] - pivot_sum
        for j in finished:
            pivot_block = pivot_block - product(
                win_factor[j * width : (j + 1) * width, first_col : first_col + width].T,
                window_blocks[j, k],
            )
        window_blocks[k, k] = pivot_block
        column_store[k] = column_now
        share_store[k] = share_column
    anc_columns = jnp.concatenate([share_store[k] for k in range(steps_total)], axis=1)
    win_inverse = jnp.concatenate(
        [
            jnp.concatenate([window_blocks[i, k] for k in range(steps_total)], axis=1)
            for i in range(steps_total)
        ],
        axis=0,
    )
    return (anc_columns, win_inverse)


vmem_bytes = 60 * 1024 * 1024
tile = 128
little = pl.CostEstimate(flops=1, bytes_accessed=1, transcendentals=0)


def halves_of(value):
    high = value.astype(jnp.bfloat16)
    return high, (value - high.astype(jnp.float32)).astype(jnp.bfloat16)


def product_of(left, right, turned=False):
    dims = ((0,), (0,)) if turned else ((1,), (0,))

    def dot(a, b):
        return lax.dot_general(a, b, (dims, ((), ())), preferred_element_type=jnp.float32)

    return dot(left[0], right[0]) + dot(left[0], right[1]) + dot(left[1], right[0])


def times(left, right, turned=False):
    return product_of(halves_of(left), halves_of(right), turned)


def chip_at(place, levels):
    return jnp.where(place < levels, 2 * place, 2 * (2 * levels - 1 - place) + 1)


def ring_place(index, levels):
    z = index // 4
    return jnp.where((index // 2) % 2 == 0, z, 2 * levels - 1 - z)


def source_device(step, index, levels):
    away = jnp.where(step % 2 == 1, -((step + 1) // 2), step // 2)
    spot = lax.rem(ring_place(index, levels) + away + 2 * levels, 2 * levels)
    return 2 * chip_at(spot, levels) + index % 2


def head_kernel(width, cuts, index_ref, structure_ref, factor_ref, masked_ref, *turned_refs):
    rows, all_cols = factor_ref.shape
    share = math.gcd(rows, width)
    for t in range(rows // share):
        block = (index_ref[0] * rows + t * share) // width
        at = slice(t * share, (t + 1) * share)
        for k in range(all_cols // width):
            kept = structure_ref[k, block].astype(jnp.float32)
            cols = slice(k * width, (k + 1) * width)
            masked_ref[at, cols] = factor_ref[at, cols] * kept
    for (first, last), ref in zip(cuts, turned_refs):
        ref[...] = masked_ref[:, first:last].T


def head(index, structure, anc_factor, width, cuts):
    rows, all_cols = anc_factor.shape
    smem = pl.BlockSpec(memory_space=pltpu.SMEM)
    vmem = pl.BlockSpec(memory_space=pltpu.VMEM)
    return pl.pallas_call(
        functools.partial(head_kernel, width, cuts),
        in_specs=[smem, smem, vmem],
        out_specs=[vmem] * (1 + len(cuts)),
        out_shape=[jax.ShapeDtypeStruct((rows, all_cols), jnp.float32)]
        + [jax.ShapeDtypeStruct((last - first, rows), jnp.float32) for first, last in cuts],
        compiler_params=pltpu.CompilerParams(vmem_limit_bytes=vmem_bytes),
        cost_estimate=little,
    )(index, structure, anc_factor)


def multiply_kernel(layout, has_start, rows_at, index_ref, *refs):
    refs = list(refs)
    sources = [refs.pop(0) for _ in range(4)]
    piece_count = sum(len(block) for block in layout)
    pieces = [refs.pop(0) for _ in range(piece_count)]
    starts = [refs.pop(0) for _ in range(2)] if has_start else None
    factors = [refs.pop(0) for _ in range(2)] if rows_at else None
    outs = [refs.pop(0) for _ in range(2)]
    inner_ref = refs.pop(0) if rows_at else None
    held = refs.pop(0)
    rows = sources[0].shape[1]
    step = pl.program_id(0)
    at = 0
    for b, block in enumerate(layout):
        chosen = pieces[at : at + len(block)]
        at += len(block)
        left = (b % 2) * rows

        @pl.when(step == b // 2)
        def _(chosen=chosen, block=block, left=left):
            for ref, (top, height) in zip(chosen, block):
                held[top : top + height, left : left + rows] = ref[...]

    @pl.when(step == 0)
    def _():
        for i in range(2):
            outs[i][...] = starts[i][...] if has_start else jnp.zeros_like(outs[i])

    inverse = jnp.concatenate(
        [
            jnp.concatenate([own[...], twin[...]], axis=1)
            for own, twin in (sources[:2], sources[2:])
        ],
        axis=0,
    )
    value = product_of(halves_of(held[...]), halves_of(inverse))
    for i in range(2):
        outs[i][...] += value[:, i * rows : (i + 1) * rows]
    if rows_at:

        @pl.when(step == len(layout) // 2 - 1)
        def _():
            image = halves_of(jnp.concatenate([out[...] for out in outs], axis=1))
            side = halves_of(jnp.concatenate([ref[...] for ref in factors], axis=0))
            spot = 0
            for start in range(0, len(rows_at), 2):
                group = rows_at[start : start + 2]
                top, last = group[0][0], group[-1][1] + tile
                value = product_of(
                    tuple(half[top : top + len(group) * tile] for half in image),
                    tuple(half[:, :last] for half in side),
                )
                for place, (_, first) in enumerate(group):
                    for i in range(first // tile + 1):
                        inner_ref[spot * tile : (spot + 1) * tile, :] = value[
                            place * tile : (place + 1) * tile, i * tile : (i + 1) * tile
                        ]
                        spot += 1


def multiply(index, inverse, twin, first, blocks, start=None, rows_at=(), factors=()):
    rows = inverse.shape[1]
    levels = inverse.shape[0] // rows // 4
    layout, flat = [], []
    for block in blocks:
        top, places = 0, []
        for piece in block:
            places.append((top, piece.shape[0]))
            top += piece.shape[0]
            flat.append(piece)
        layout.append(tuple(places))
    height = top

    def whole(shape):
        return pl.BlockSpec(shape, lambda i, at: (0, 0))

    def source(side):
        return pl.BlockSpec(
            (rows, rows), lambda i, at: (source_device(first + 2 * i + side, at[0], levels), 0)
        )

    image = jax.ShapeDtypeStruct((height, rows), jnp.float32)
    out_shape = [image, image]
    if rows_at:
        count = sum(first // tile + 1 for _, first in rows_at)
        out_shape.append(jax.ShapeDtypeStruct((count * tile, tile), jnp.float32))
    operands = flat + list(start or ()) + list(factors)
    return pl.pallas_call(
        functools.partial(multiply_kernel, tuple(layout), start is not None, rows_at),
        grid_spec=pltpu.PrefetchScalarGridSpec(
            num_scalar_prefetch=1,
            grid=(len(blocks) // 2,),
            in_specs=[source(0), source(0), source(1), source(1)]
            + [whole(v.shape) for v in flat + list(start or ())]
            + [whole((rows, rows_at[-1][1] + tile)) for _ in factors],
            out_specs=[whole(v.shape) for v in out_shape],
            scratch_shapes=[pltpu.VMEM((height, 2 * rows), jnp.float32)],
        ),
        out_shape=out_shape,
        compiler_params=pltpu.CompilerParams(vmem_limit_bytes=vmem_bytes),
        cost_estimate=little,
    )(index, inverse, twin, inverse, twin, *operands)


def columns_kernel(width, steps, image_ref, add_ref, factor_ref, out_ref):
    solved = {}
    for k in range(steps - 1, -1, -1):
        if k:
            at = slice((k - 1) * width, k * width)
            value = image_ref[at, :] + add_ref[at, :]
        else:
            value = jnp.zeros((width, image_ref.shape[1]), jnp.float32)
        for j in range(k + 1, steps):
            side = factor_ref[j * width : (j + 1) * width, k * width : (k + 1) * width]
            value = value + times(side, solved[j], True)
        solved[k] = -value
        out_ref[:, k * width : (k + 1) * width] = solved[k].T


def solve_columns(width, steps, image, add, win_factor):
    rows = image.shape[1]
    return pl.pallas_call(
        functools.partial(columns_kernel, width, steps),
        out_shape=jax.ShapeDtypeStruct((rows, steps * width), jnp.float32),
        compiler_params=pltpu.CompilerParams(vmem_limit_bytes=vmem_bytes),
        cost_estimate=little,
    )(image, add, win_factor)


def fill_inner(inner, top, one, two, first_half):
    whole = jnp.concatenate(
        [jnp.where(first_half, one, two), jnp.where(first_half, two, one)], axis=0
    )
    spot, row = 0, top
    while spot * tile < whole.shape[0]:
        for i in range(row // tile + 1):
            block = whole[spot * tile : (spot + 1) * tile]
            spot += 1
            inner[row : row + tile, i * tile : (i + 1) * tile] = block
            if i * tile < row:
                inner[i * tile : (i + 1) * tile, row : row + tile] = block.T
        row += tile


def last_kernel(
    core_ref, mine_ref, other_ref, image_ref, add_ref, columns_ref, base_ref, *refs
):
    columns_out, window_out, inner = refs
    columns_out[...] = columns_ref[...] - (image_ref[...] + add_ref[...]).T
    fill_inner(inner, 0, mine_ref[...], other_ref[...], core_ref[0] % 2 == 0)
    window_out[...] = base_ref[...] + inner[...]


def add_last(index, mine, other, image, add, columns, base):
    width, rows = image.shape
    column_block = pl.BlockSpec((rows, width), lambda i: (0, 0))
    window_block = pl.BlockSpec((width, width), lambda i: (0, 0))
    part = pl.BlockSpec(mine.shape, lambda i: (0, 0))
    whole = pl.BlockSpec(image.shape, lambda i: (0, 0))
    return pl.pallas_call(
        last_kernel,
        grid=(1,),
        in_specs=[pl.BlockSpec(memory_space=pltpu.SMEM), part, part, whole, whole]
        + [column_block, window_block],
        out_specs=[column_block, window_block],
        out_shape=[
            jax.ShapeDtypeStruct(columns.shape, jnp.float32),
            jax.ShapeDtypeStruct(base.shape, jnp.float32),
        ],
        input_output_aliases={5: 0, 6: 1},
        scratch_shapes=[pltpu.VMEM((width, width), jnp.float32)],
        compiler_params=pltpu.CompilerParams(vmem_limit_bytes=vmem_bytes),
        cost_estimate=little,
    )(index, mine, other, image, add, columns, base)


def window_kernel(width, steps, tops, core_ref, *refs):
    mine, other = refs[: len(tops)], refs[len(tops) : 2 * len(tops)]
    factor_ref, pivot_ref, out_ref, inner = refs[2 * len(tops) :]
    low = min(tops)
    if low:
        inner[:low, :low] = jnp.zeros((low, low), jnp.float32)
    for top, mine_ref, other_ref in zip(tops, mine, other):
        fill_inner(inner, top, mine_ref[...], other_ref[...], core_ref[0] % 2 == 0)

    def at(k):
        return slice(k * width, (k + 1) * width)

    cross = {}
    for k in range(steps - 1, -1, -1):
        later = range(k + 1, steps)
        for i in range(k + 1):
            value = inner[at(k), at(i)]
            for j in later:
                value = value + times(factor_ref[at(j), at(k)], cross[j, i], True)
            cross[k, i] = -value
        for j in later:
            value = cross[j, k]
            for i in later:
                value = value + times(out_ref[at(j), at(i)], factor_ref[at(i), at(k)])
            out_ref[at(j), at(k)] = -value
            out_ref[at(k), at(j)] = -value.T
        value = pivot_ref[k] - cross[k, k].T
        for j in later:
            value = value - times(factor_ref[at(j), at(k)], out_ref[at(j), at(k)], True)
        out_ref[at(k), at(k)] = value


def window_blocks_of(width, steps, tops, index, mine, other, win_factor, pivot_inverse):
    order = steps * width
    vmem = pl.BlockSpec(memory_space=pltpu.VMEM)
    count = 2 * len(tops) + 2
    return pl.pallas_call(
        functools.partial(window_kernel, width, steps, tops),
        in_specs=[pl.BlockSpec(memory_space=pltpu.SMEM)] + [vmem] * count,
        out_specs=vmem,
        out_shape=jax.ShapeDtypeStruct((order, order), jnp.float32),
        scratch_shapes=[pltpu.VMEM((order, order), jnp.float32)],
        compiler_params=pltpu.CompilerParams(vmem_limit_bytes=vmem_bytes),
        cost_estimate=little,
    )(index, *mine, *other, win_factor, pivot_inverse)


def fast(anc_inverse, anc_factor, win_factor, pivot_inverse, structure):
    n = lax.axis_size("pcol")
    index = lax.axis_index("pcol")
    levels = n // 4
    chips = n // 2
    half_way = chips // 2
    core = index % 2
    x = (index // 2) % 2
    z = index // 4
    rows = anc_inverse.shape[1]
    steps_total, width = pivot_inverse.shape[:2]
    all_cols = anc_factor.shape[1]
    order = [2 * s if s < levels else 2 * (chips - 1 - s) + 1 for s in range(chips)]
    forward = [
        (2 * order[s] + c, 2 * order[(s + 1) % chips] + c) for s in range(chips) for c in range(2)
    ]
    backward = [(to, start) for start, to in forward]

    def flip(bits):
        return [(p, p ^ bits) for p in range(n)]

    def send(value, pairs):
        return lax.ppermute(value, "pcol", pairs)

    def pick(value, at):
        return lax.dynamic_index_in_dim(value, at, 0, keepdims=False)

    def swap_halves(value, bit):
        halves = value.reshape((2, value.shape[0] // 2) + value.shape[1:])
        return pick(halves, bit), pick(halves, 1 - bit)

    def join(bit, mine, other):
        return jnp.concatenate(
            [jnp.where(bit == 0, mine, other), jnp.where(bit == 0, other, mine)], axis=0
        )

    def sum_small(value):
        mine, other = swap_halves(value, core)
        got = yield [send(other, flip(1))]
        mine = mine + got[0]
        got = yield [send(mine, flip(2))]
        mine = mine + got[0]
        got = yield [send(mine, flip(4 * d)) for d in range(1, levels)]
        for value in got:
            mine = mine + value
        got = yield [send(mine, flip(1))]
        yield mine, got[0]

    def sum_large(value):
        mine, other = swap_halves(value, core)
        got = yield [send(other, flip(1))]
        mine, other = swap_halves(mine + got[0], x)
        got = yield [send(other, flip(2))]
        mine = mine + got[0]
        parts = mine.reshape((levels, mine.shape[0] // levels) + mine.shape[1:])
        got = yield [send(pick(parts, z ^ d), flip(4 * d)) for d in range(1, levels)]
        total = pick(parts, z)
        for value in got:
            total = total + value
        got = yield [send(total, flip(4 * d)) for d in range(1, levels)]
        pieces = [total] + got
        bit = 1
        while bit < levels:
            pieces = [
                join((z // bit) % 2, pieces[i], pieces[i + 1]) for i in range(0, len(pieces), 2)
            ]
            bit *= 2
        mine = pieces[0]
        got = yield [send(mine, flip(2))]
        mine = join(x, mine, got[0])
        got = yield [send(mine, flip(1))]
        yield mine, got[0]

    def ends(up, down):
        middle = up.shape[0] // 2
        return [send(up[:middle], forward), send(down[middle:], backward)]

    at = index.astype(jnp.int32).reshape(1)
    plan = (((width, 2 * width), (2 * width, all_cols)), ((0, width),))
    cuts = tuple(cut for streams in plan for cut in streams)
    factor, *turned = head(at, structure, anc_factor, width, cuts)
    twin = send(anc_inverse, flip(1))
    factor_twin = send(factor, flip(1))
    factors = (factor, factor_twin)

    def ring(pieces):
        ups = downs = list(pieces)
        yield ups, ups
        for s in range(1, half_way):
            ups = [send(v, forward) for v in ups]
            downs = [send(v, backward) for v in downs]
            ups, downs = yield ups, downs
        if len(ups) == 2:
            yield [send(ups[0], forward), send(downs[1], backward)]
        else:
            yield ends(ups[0], downs[0])

    def strips(streams):
        first, last = streams[0][0], streams[-1][1]
        return tuple((i - first, i) for i in range(first, last, tile))

    def product(start, blocks, total=None, rows_at=()):
        return multiply(
            at, anc_inverse, twin, start, blocks, total, rows_at, factors if rows_at else ()
        )

    hold = lax.optimization_barrier
    ring_a = ring(turned[: len(plan[0])])
    pieces_b = turned[len(plan[0]) :]
    a = [next(ring_a)[0]]
    ups_a, downs_a = next(ring_a)
    a += [ups_a, downs_a]
    ups_a, downs_a = ring_a.send((ups_a, downs_a))
    a += [ups_a, downs_a]
    ups_a, downs_a = ring_a.send((ups_a, downs_a))
    near = product(0, a[:4])
    (ups_a, downs_a), near = hold(((ups_a, downs_a), near))
    pieces_b, downs_a = hold((pieces_b, downs_a))
    far = ring_a.send((ups_a, downs_a))
    a += [ups_a, downs_a, far]
    ring_b = ring(pieces_b)
    b = [next(ring_b)[0]]
    ups_b, downs_b = next(ring_b)
    mid = product(4, a[4:6], near)
    mine_a, theirs_a, local = product(6, a[6:], mid, strips(plan[0]))
    (ups_b, downs_b), local = hold(((ups_b, downs_b), local))
    sum_a = sum_large(local)
    got = next(sum_a)
    got = sum_a.send(got)
    b += [ups_b, downs_b]
    ups_b, downs_b = ring_b.send((ups_b, downs_b))
    adds_a = send(theirs_a, flip(1))
    b += [ups_b, downs_b]
    near = product(0, b[:4])
    (ups_b, downs_b), got, near = hold(((ups_b, downs_b), got, near))
    got = sum_a.send(got)
    ups_b, downs_b = ring_b.send((ups_b, downs_b))
    b += [ups_b, downs_b]
    mid = product(4, b[4:6], near)
    columns = solve_columns(width, steps_total, mine_a, adds_a, win_factor)
    got, mid, columns = hold((got, mid, columns))
    got = sum_a.send(got)
    b += [ring_b.send((ups_b, downs_b))]
    mine_b, theirs_b, local = product(6, b[6:], mid, strips(plan[1]))
    adds_b = send(theirs_b, flip(1))
    sum_b = sum_small(local)
    got_b = next(sum_b)
    got = sum_a.send(got)
    got_b, got = hold((got_b, got))
    got_b = sum_b.send(got_b)
    got = sum_a.send(got)
    got_b, got = hold((got_b, got))
    got_b = sum_b.send(got_b)
    mine, other = sum_a.send(got)
    base = window_blocks_of(
        width, steps_total, (width,), at, [mine], [other], win_factor, pivot_inverse
    )
    got_b, base = hold((got_b, base))
    got_b = sum_b.send(got_b)
    anc_columns, win_inverse = add_last(
        at, *sum_b.send(got_b), mine_b, adds_b, columns, base
    )
    return (anc_columns, win_inverse)


def solution(mesh):
    in_specs = (
        P(("pole", "prow"), "pcol"),
        P(("pole", "pcol"), None),
        P("pole", None),
        P("pole", None, None),
        P(),
    )
    out_specs = (P(("pole", "prow", "pcol"), None), P("pole", None))
    levels = mesh.shape["pcol"] // 4
    ringed = mesh.shape["prow"] == 1 and mesh.shape["pcol"] % 4 == 0
    ringed = ringed and levels > 1 and levels & (levels - 1) == 0
    return jax.shard_map(
        fast if ringed else on_device, mesh=mesh, in_specs=in_specs, out_specs=out_specs, check_vma=False
    )
```

```python
import functools
import math

import jax
import jax.numpy as jnp
from jax import lax
from jax.experimental import pallas as pl
from jax.experimental.pallas import tpu as pltpu
from jax.sharding import PartitionSpec as P

precise = lax.Precision.HIGHEST


def product(left, right):
    return jnp.dot(left, right, precision=precise, preferred_element_type=jnp.float32)


def on_device(anc_inverse, anc_factor, win_factor, pivot_inverse, structure):
    row_count = lax.axis_size("prow")
    col_count = lax.axis_size("pcol")
    row_index = lax.axis_index("prow")
    col_index = lax.axis_index("pcol")
    block_rows = anc_inverse.shape[0]
    block_cols = anc_inverse.shape[1]
    steps_total = pivot_inverse.shape[0]
    width = pivot_inverse.shape[1]
    all_cols = anc_factor.shape[1]
    block_count = structure.shape[1]
    ratio_cols = col_count // row_count
    share_rows = block_rows // col_count
    structure_cols = structure.T.astype(jnp.float32)
    global_rows = col_index * block_cols + lax.iota(jnp.int32, block_cols)
    onehot_rows = (
        (global_rows // width)[:, None] == lax.iota(jnp.int32, block_count)[None, :]
    ).astype(jnp.float32)
    kept_rows = product(onehot_rows, structure_cols)
    share_offset = col_index * share_rows
    share_global = (row_index * col_count + col_index) * share_rows + lax.iota(
        jnp.int32, share_rows
    )
    onehot_share = (
        (share_global // width)[:, None] == lax.iota(jnp.int32, block_count)[None, :]
    ).astype(jnp.float32)
    kept_share = product(onehot_share, structure_cols)
    slot_ids = lax.iota(jnp.int32, col_count)
    source_flag = (slot_ids // row_count == col_index - row_index * ratio_cols).astype(jnp.float32)
    pieces = jnp.tile(anc_factor.reshape(row_count, share_rows, all_cols), (ratio_cols, 1, 1))
    outgoing = pieces * source_flag[:, None, None]
    incoming = lax.all_to_all(outgoing, "pcol", split_axis=0, concat_axis=0, tiled=True)
    factor_share = jnp.sum(incoming, axis=0)
    column_store = {}
    share_store = {}
    window_blocks = {}
    for k in range(steps_total - 1, -1, -1):
        first_col = k * width
        factor_now = anc_factor[:, first_col : first_col + width] * kept_rows[:, k : k + 1]
        share_factor = factor_share[:, first_col : first_col + width] * kept_share[:, k : k + 1]
        finished = list(range(k + 1, steps_total))
        if finished:
            stacked = jnp.concatenate([column_store[j] for j in finished], axis=1)
            factor_win = win_factor[first_col + width :, first_col : first_col + width]

        def term_rows(start, count, factor_now=factor_now):
            return product(anc_inverse, factor_now)

        share_image = lax.psum_scatter(
            term_rows(jnp.int32(0), share_rows * lax.axis_size("pcol")),
            "pcol",
            scatter_dimension=0,
            tiled=True,
        )
        if finished:
            share_image = share_image + product(
                lax.dynamic_slice_in_dim(stacked, share_offset, share_rows, 0), factor_win
            )
        share_column = -share_image
        column_now = lax.all_gather(share_column, "pcol", axis=0, tiled=True)
        crossings = [product(share_store[j].T, share_factor) for j in finished]
        pivot_part = product(share_factor.T, share_column)
        cross_sums = []
        if finished:
            cross_total = lax.psum(jnp.stack(crossings), ("prow", "pcol"))
            cross_sums = [cross_total[position] for position in range(len(finished))]
        pivot_sum = lax.psum(pivot_part, ("prow", "pcol"))
        for position, j in enumerate(finished):
            running = cross_sums[position]
            for i in finished:
                running = running + product(
                    window_blocks[j, i],
                    win_factor[i * width : (i + 1) * width, first_col : first_col + width],
                )
            window_blocks[j, k] = -running
            window_blocks[k, j] = -running.T
        pivot_block = pivot_inverse[k] - pivot_sum
        for j in finished:
            pivot_block = pivot_block - product(
                win_factor[j * width : (j + 1) * width, first_col : first_col + width].T,
                window_blocks[j, k],
            )
        window_blocks[k, k] = pivot_block
        column_store[k] = column_now
        share_store[k] = share_column
    anc_columns = jnp.concatenate([share_store[k] for k in range(steps_total)], axis=1)
    win_inverse = jnp.concatenate(
        [
            jnp.concatenate([window_blocks[i, k] for k in range(steps_total)], axis=1)
            for i in range(steps_total)
        ],
        axis=0,
    )
    return (anc_columns, win_inverse)


vmem_bytes = 60 * 1024 * 1024
tile = 128
little = pl.CostEstimate(flops=1, bytes_accessed=1, transcendentals=0)


def halves_of(value):
    high = value.astype(jnp.bfloat16)
    return high, (value - high.astype(jnp.float32)).astype(jnp.bfloat16)


def product_of(left, right, turned=False):
    dims = ((0,), (0,)) if turned else ((1,), (0,))

    def dot(a, b):
        return lax.dot_general(a, b, (dims, ((), ())), preferred_element_type=jnp.float32)

    return dot(left[0], right[0]) + dot(left[0], right[1]) + dot(left[1], right[0])


def times(left, right, turned=False):
    return product_of(halves_of(left), halves_of(right), turned)


def chip_at(place, levels):
    return jnp.where(place < levels, 2 * place, 2 * (2 * levels - 1 - place) + 1)


def ring_place(index, levels):
    z = index // 4
    return jnp.where((index // 2) % 2 == 0, z, 2 * levels - 1 - z)


def source_device(step, index, levels):
    away = jnp.where(step % 2 == 1, -((step + 1) // 2), step // 2)
    spot = lax.rem(ring_place(index, levels) + away + 2 * levels, 2 * levels)
    return 2 * chip_at(spot, levels) + index % 2


def head_kernel(width, cuts, index_ref, structure_ref, factor_ref, masked_ref, *turned_refs):
    rows, all_cols = factor_ref.shape
    share = math.gcd(rows, width)
    for t in range(rows // share):
        block = (index_ref[0] * rows + t * share) // width
        at = slice(t * share, (t + 1) * share)
        for k in range(all_cols // width):
            kept = structure_ref[k, block].astype(jnp.float32)
            cols = slice(k * width, (k + 1) * width)
            masked_ref[at, cols] = factor_ref[at, cols] * kept
    for (first, last), ref in zip(cuts, turned_refs):
        ref[...] = masked_ref[:, first:last].T


def head(index, structure, anc_factor, width, cuts):
    rows, all_cols = anc_factor.shape
    smem = pl.BlockSpec(memory_space=pltpu.SMEM)
    vmem = pl.BlockSpec(memory_space=pltpu.VMEM)
    return pl.pallas_call(
        functools.partial(head_kernel, width, cuts),
        in_specs=[smem, smem, vmem],
        out_specs=[vmem] * (1 + len(cuts)),
        out_shape=[jax.ShapeDtypeStruct((rows, all_cols), jnp.float32)]
        + [jax.ShapeDtypeStruct((last - first, rows), jnp.float32) for first, last in cuts],
        compiler_params=pltpu.CompilerParams(vmem_limit_bytes=vmem_bytes),
        cost_estimate=little,
    )(index, structure, anc_factor)


def multiply_kernel(layout, has_start, rows_at, index_ref, *refs):
    refs = list(refs)
    late = []
    if rows_at:
        sem = refs.pop()
        kept = [refs.pop() for _ in range(4)][::-1]
    sources = [refs.pop(0) for _ in range(4)]
    piece_count = sum(len(block) for block in layout)
    pieces = [refs.pop(0) for _ in range(piece_count)]
    starts = [refs.pop(0) for _ in range(2)] if has_start else None
    factors = [refs.pop(0) for _ in range(2)] if rows_at else None
    outs = [refs.pop(0) for _ in range(2)]
    inner_ref = refs.pop(0) if rows_at else None
    held = refs.pop(0)
    rows = sources[0].shape[1]
    step = pl.program_id(0)
    if rows_at:
        last = rows_at[-1][1] + tile
        away = starts + [ref.at[:, pl.ds(0, last)] for ref in factors]
        late = [
            pltpu.make_async_copy(ref, place, sem.at[i])
            for i, (ref, place) in enumerate(zip(away, kept))
        ]
        for copy in late:
            copy.start()
        starts, factors = kept[:2], kept[2:]
    at = 0
    for b, block in enumerate(layout):
        chosen = pieces[at : at + len(block)]
        at += len(block)
        left = (b % 2) * rows

        @pl.when(step == b // 2)
        def _(chosen=chosen, block=block, left=left):
            for ref, (top, height) in zip(chosen, block):
                held[top : top + height, left : left + rows] = ref[...]

    if not rows_at:

        @pl.when(step == 0)
        def _():
            for i in range(2):
                outs[i][...] = starts[i][...] if has_start else jnp.zeros_like(outs[i])

    inverse = jnp.concatenate(
        [
            jnp.concatenate([own[...], twin[...]], axis=1)
            for own, twin in (sources[:2], sources[2:])
        ],
        axis=0,
    )
    value = product_of(halves_of(held[...]), halves_of(inverse))
    for copy in late[:2]:
        copy.wait()
    for i in range(2):
        before = starts[i] if rows_at else outs[i]
        outs[i][...] = before[...] + value[:, i * rows : (i + 1) * rows]
    for copy in late[2:]:
        copy.wait()
    if rows_at:

        @pl.when(step == len(layout) // 2 - 1)
        def _():
            image = halves_of(jnp.concatenate([out[...] for out in outs], axis=1))
            side = halves_of(jnp.concatenate([ref[...] for ref in factors], axis=0))
            spot = 0
            for start in range(0, len(rows_at), 2):
                group = rows_at[start : start + 2]
                top, last = group[0][0], group[-1][1] + tile
                value = product_of(
                    tuple(half[top : top + len(group) * tile] for half in image),
                    tuple(half[:, :last] for half in side),
                )
                for place, (_, first) in enumerate(group):
                    for i in range(first // tile + 1):
                        inner_ref[spot * tile : (spot + 1) * tile, :] = value[
                            place * tile : (place + 1) * tile, i * tile : (i + 1) * tile
                        ]
                        spot += 1


def multiply(index, inverse, twin, first, blocks, start=None, rows_at=(), factors=()):
    rows = inverse.shape[1]
    levels = inverse.shape[0] // rows // 4
    layout, flat = [], []
    for block in blocks:
        top, places = 0, []
        for piece in block:
            places.append((top, piece.shape[0]))
            top += piece.shape[0]
            flat.append(piece)
        layout.append(tuple(places))
    height = top

    def whole(shape):
        return pl.BlockSpec(shape, lambda i, at: (0, 0))

    def source(side):
        return pl.BlockSpec(
            (rows, rows), lambda i, at: (source_device(first + 2 * i + side, at[0], levels), 0)
        )

    image = jax.ShapeDtypeStruct((height, rows), jnp.float32)
    out_shape = [image, image]
    if rows_at:
        count = sum(first // tile + 1 for _, first in rows_at)
        out_shape.append(jax.ShapeDtypeStruct((count * tile, tile), jnp.float32))
    operands = flat + list(start or ()) + list(factors)
    scratch = []
    if rows_at:
        shapes = [(height, rows)] * 2 + [(rows, rows_at[-1][1] + tile)] * 2
        scratch = [pltpu.VMEM(shape, jnp.float32) for shape in shapes]
        scratch.append(pltpu.SemaphoreType.DMA((4,)))
    return pl.pallas_call(
        functools.partial(multiply_kernel, tuple(layout), start is not None, rows_at),
        grid_spec=pltpu.PrefetchScalarGridSpec(
            num_scalar_prefetch=1,
            grid=(len(blocks) // 2,),
            in_specs=[source(0), source(0), source(1), source(1)]
            + [whole(v.shape) for v in flat]
            + [pl.BlockSpec(memory_space=pl.ANY) if rows_at else whole(v.shape) for v in start or ()]
            + [pl.BlockSpec(memory_space=pl.ANY) for _ in factors],
            out_specs=[whole(v.shape) for v in out_shape],
            scratch_shapes=[pltpu.VMEM((height, 2 * rows), jnp.float32)] + scratch,
        ),
        out_shape=out_shape,
        compiler_params=pltpu.CompilerParams(vmem_limit_bytes=vmem_bytes),
        cost_estimate=little,
    )(index, inverse, twin, inverse, twin, *operands)


def columns_kernel(width, steps, image_ref, add_ref, factor_ref, out_ref):
    solved = {}
    for k in range(steps - 1, -1, -1):
        if k:
            at = slice((k - 1) * width, k * width)
            value = image_ref[at, :] + add_ref[at, :]
        else:
            value = jnp.zeros((width, image_ref.shape[1]), jnp.float32)
        for j in range(k + 1, steps):
            side = factor_ref[j * width : (j + 1) * width, k * width : (k + 1) * width]
            value = value + times(side, solved[j], True)
        solved[k] = -value
        out_ref[:, k * width : (k + 1) * width] = solved[k].T


def solve_columns(width, steps, image, add, win_factor):
    rows = image.shape[1]
    return pl.pallas_call(
        functools.partial(columns_kernel, width, steps),
        out_shape=jax.ShapeDtypeStruct((rows, steps * width), jnp.float32),
        compiler_params=pltpu.CompilerParams(vmem_limit_bytes=vmem_bytes),
        cost_estimate=little,
    )(image, add, win_factor)


def fill_inner(inner, top, one, two, first_half):
    whole = jnp.concatenate(
        [jnp.where(first_half, one, two), jnp.where(first_half, two, one)], axis=0
    )
    spot, row = 0, top
    while spot * tile < whole.shape[0]:
        for i in range(row // tile + 1):
            block = whole[spot * tile : (spot + 1) * tile]
            spot += 1
            inner[row : row + tile, i * tile : (i + 1) * tile] = block
            if i * tile < row:
                inner[i * tile : (i + 1) * tile, row : row + tile] = block.T
        row += tile


def last_kernel(
    core_ref, mine_ref, other_ref, image_ref, add_ref, columns_ref, base_ref, *refs
):
    columns_out, window_out, inner = refs
    columns_out[...] = columns_ref[...] - (image_ref[...] + add_ref[...]).T
    fill_inner(inner, 0, mine_ref[...], other_ref[...], core_ref[0] % 2 == 0)
    window_out[...] = base_ref[...] + inner[...]


def add_last(index, mine, other, image, add, columns, base):
    width, rows = image.shape
    column_block = pl.BlockSpec((rows, width), lambda i: (0, 0))
    window_block = pl.BlockSpec((width, width), lambda i: (0, 0))
    part = pl.BlockSpec(mine.shape, lambda i: (0, 0))
    whole = pl.BlockSpec(image.shape, lambda i: (0, 0))
    return pl.pallas_call(
        last_kernel,
        grid=(1,),
        in_specs=[pl.BlockSpec(memory_space=pltpu.SMEM), part, part, whole, whole]
        + [column_block, window_block],
        out_specs=[column_block, window_block],
        out_shape=[
            jax.ShapeDtypeStruct(columns.shape, jnp.float32),
            jax.ShapeDtypeStruct(base.shape, jnp.float32),
        ],
        input_output_aliases={5: 0, 6: 1},
        scratch_shapes=[pltpu.VMEM((width, width), jnp.float32)],
        compiler_params=pltpu.CompilerParams(vmem_limit_bytes=vmem_bytes),
        cost_estimate=little,
    )(index, mine, other, image, add, columns, base)


def window_kernel(width, steps, tops, core_ref, *refs):
    mine, other = refs[: len(tops)], refs[len(tops) : 2 * len(tops)]
    factor_ref, pivot_ref, out_ref, inner = refs[2 * len(tops) :]
    low = min(tops)
    if low:
        inner[:low, :low] = jnp.zeros((low, low), jnp.float32)
    for top, mine_ref, other_ref in zip(tops, mine, other):
        fill_inner(inner, top, mine_ref[...], other_ref[...], core_ref[0] % 2 == 0)

    def at(k):
        return slice(k * width, (k + 1) * width)

    cross = {}
    for k in range(steps - 1, -1, -1):
        later = range(k + 1, steps)
        for i in range(k + 1):
            value = inner[at(k), at(i)]
            for j in later:
                value = value + times(factor_ref[at(j), at(k)], cross[j, i], True)
            cross[k, i] = -value
        for j in later:
            value = cross[j, k]
            for i in later:
                value = value + times(out_ref[at(j), at(i)], factor_ref[at(i), at(k)])
            out_ref[at(j), at(k)] = -value
            out_ref[at(k), at(j)] = -value.T
        value = pivot_ref[k] - cross[k, k].T
        for j in later:
            value = value - times(factor_ref[at(j), at(k)], out_ref[at(j), at(k)], True)
        out_ref[at(k), at(k)] = value


def window_blocks_of(width, steps, tops, index, mine, other, win_factor, pivot_inverse):
    order = steps * width
    vmem = pl.BlockSpec(memory_space=pltpu.VMEM)
    count = 2 * len(tops) + 2
    return pl.pallas_call(
        functools.partial(window_kernel, width, steps, tops),
        in_specs=[pl.BlockSpec(memory_space=pltpu.SMEM)] + [vmem] * count,
        out_specs=vmem,
        out_shape=jax.ShapeDtypeStruct((order, order), jnp.float32),
        scratch_shapes=[pltpu.VMEM((order, order), jnp.float32)],
        compiler_params=pltpu.CompilerParams(vmem_limit_bytes=vmem_bytes),
        cost_estimate=little,
    )(index, *mine, *other, win_factor, pivot_inverse)


def fast(anc_inverse, anc_factor, win_factor, pivot_inverse, structure):
    n = lax.axis_size("pcol")
    index = lax.axis_index("pcol")
    levels = n // 4
    chips = n // 2
    half_way = chips // 2
    core = index % 2
    x = (index // 2) % 2
    z = index // 4
    rows = anc_inverse.shape[1]
    steps_total, width = pivot_inverse.shape[:2]
    all_cols = anc_factor.shape[1]
    order = [2 * s if s < levels else 2 * (chips - 1 - s) + 1 for s in range(chips)]
    forward = [
        (2 * order[s] + c, 2 * order[(s + 1) % chips] + c) for s in range(chips) for c in range(2)
    ]
    backward = [(to, start) for start, to in forward]

    def flip(bits):
        return [(p, p ^ bits) for p in range(n)]

    def send(value, pairs):
        return lax.ppermute(value, "pcol", pairs)

    def pick(value, at):
        return lax.dynamic_index_in_dim(value, at, 0, keepdims=False)

    def swap_halves(value, bit):
        halves = value.reshape((2, value.shape[0] // 2) + value.shape[1:])
        return pick(halves, bit), pick(halves, 1 - bit)

    def join(bit, mine, other):
        return jnp.concatenate(
            [jnp.where(bit == 0, mine, other), jnp.where(bit == 0, other, mine)], axis=0
        )

    def sum_small(value):
        mine, other = swap_halves(value, core)
        got = yield [send(other, flip(1))]
        mine = mine + got[0]
        got = yield [send(mine, flip(2))]
        mine = mine + got[0]
        got = yield [send(mine, flip(4 * d)) for d in range(1, levels)]
        for value in got:
            mine = mine + value
        got = yield [send(mine, flip(1))]
        yield mine, got[0]

    def sum_large(value):
        mine, other = swap_halves(value, core)
        got = yield [send(other, flip(1))]
        mine, other = swap_halves(mine + got[0], x)
        got = yield [send(other, flip(2))]
        mine = mine + got[0]
        parts = mine.reshape((levels, mine.shape[0] // levels) + mine.shape[1:])
        got = yield [send(pick(parts, z ^ d), flip(4 * d)) for d in range(1, levels)]
        total = pick(parts, z)
        for value in got:
            total = total + value
        got = yield [send(total, flip(4 * d)) for d in range(1, levels)]
        pieces = [total] + got
        bit = 1
        while bit < levels:
            pieces = [
                join((z // bit) % 2, pieces[i], pieces[i + 1]) for i in range(0, len(pieces), 2)
            ]
            bit *= 2
        mine = pieces[0]
        got = yield [send(mine, flip(2))]
        mine = join(x, mine, got[0])
        got = yield [send(mine, flip(1))]
        yield mine, got[0]

    def ends(up, down):
        middle = up.shape[0] // 2
        return [send(up[:middle], forward), send(down[middle:], backward)]

    at = index.astype(jnp.int32).reshape(1)
    plan = (((width, 2 * width), (2 * width, all_cols)), ((0, width),))
    cuts = tuple(cut for streams in plan for cut in streams)
    factor, *turned = head(at, structure, anc_factor, width, cuts)
    twin = send(anc_inverse, flip(1))
    factor_twin = send(factor, flip(1))
    factors = (factor, factor_twin)

    def ring(pieces):
        ups = downs = list(pieces)
        yield ups, ups
        for s in range(1, half_way):
            ups = [send(v, forward) for v in ups]
            downs = [send(v, backward) for v in downs]
            ups, downs = yield ups, downs
        if len(ups) == 2:
            yield [send(ups[0], forward), send(downs[1], backward)]
        else:
            yield ends(ups[0], downs[0])

    def strips(streams):
        first, last = streams[0][0], streams[-1][1]
        return tuple((i - first, i) for i in range(first, last, tile))

    def product(start, blocks, total=None, rows_at=()):
        return multiply(
            at, anc_inverse, twin, start, blocks, total, rows_at, factors if rows_at else ()
        )

    hold = lax.optimization_barrier
    ring_a = ring(turned[: len(plan[0])])
    pieces_b = turned[len(plan[0]) :]
    a = [next(ring_a)[0]]
    ups_a, downs_a = next(ring_a)
    a += [ups_a, downs_a]
    ups_a, downs_a = ring_a.send((ups_a, downs_a))
    a += [ups_a, downs_a]
    ups_a, downs_a = ring_a.send((ups_a, downs_a))
    near = product(0, a[:4])
    (ups_a, downs_a), near = hold(((ups_a, downs_a), near))
    pieces_b, downs_a = hold((pieces_b, downs_a))
    far = ring_a.send((ups_a, downs_a))
    a += [ups_a, downs_a, far]
    ring_b = ring(pieces_b)
    b = [next(ring_b)[0]]
    ups_b, downs_b = next(ring_b)
    mid = product(4, a[4:6], near)
    mine_a, theirs_a, local = product(6, a[6:], mid, strips(plan[0]))
    (ups_b, downs_b), local = hold(((ups_b, downs_b), local))
    sum_a = sum_large(local)
    got = next(sum_a)
    got = sum_a.send(got)
    b += [ups_b, downs_b]
    ups_b, downs_b = ring_b.send((ups_b, downs_b))
    adds_a = send(theirs_a, flip(1))
    b += [ups_b, downs_b]
    near = product(0, b[:4])
    (ups_b, downs_b), got, near = hold(((ups_b, downs_b), got, near))
    got = sum_a.send(got)
    ups_b, downs_b = ring_b.send((ups_b, downs_b))
    b += [ups_b, downs_b]
    mid = product(4, b[4:6], near)
    columns = solve_columns(width, steps_total, mine_a, adds_a, win_factor)
    got, mid, columns = hold((got, mid, columns))
    got = sum_a.send(got)
    b += [ring_b.send((ups_b, downs_b))]
    mine_b, theirs_b, local = product(6, b[6:], mid, strips(plan[1]))
    adds_b = send(theirs_b, flip(1))
    sum_b = sum_small(local)
    got_b = next(sum_b)
    got = sum_a.send(got)
    got_b, got = hold((got_b, got))
    got_b = sum_b.send(got_b)
    got = sum_a.send(got)
    got_b, got = hold((got_b, got))
    got_b = sum_b.send(got_b)
    mine, other = sum_a.send(got)
    base = window_blocks_of(
        width, steps_total, (width,), at, [mine], [other], win_factor, pivot_inverse
    )
    got_b, base = hold((got_b, base))
    got_b = sum_b.send(got_b)
    anc_columns, win_inverse = add_last(
        at, *sum_b.send(got_b), mine_b, adds_b, columns, base
    )
    return (anc_columns, win_inverse)


def solution(mesh):
    in_specs = (
        P(("pole", "prow"), "pcol"),
        P(("pole", "pcol"), None),
        P("pole", None),
        P("pole", None, None),
        P(),
    )
    out_specs = (P(("pole", "prow", "pcol"), None), P("pole", None))
    ringed = mesh.shape["prow"] == 1 and mesh.shape["pcol"] == 16
    return jax.shard_map(
        fast if ringed else on_device, mesh=mesh, in_specs=in_specs, out_specs=out_specs, check_vma=False
    )
```

```python
import functools
import math

import jax
import jax.numpy as jnp
from jax import lax
from jax.experimental import pallas as pl
from jax.experimental.pallas import tpu as pltpu
from jax.sharding import PartitionSpec as P

precise = lax.Precision.HIGHEST


def product(left, right):
    return jnp.dot(left, right, precision=precise, preferred_element_type=jnp.float32)


def on_device(anc_inverse, anc_factor, win_factor, pivot_inverse, structure):
    row_count = lax.axis_size("prow")
    col_count = lax.axis_size("pcol")
    row_index = lax.axis_index("prow")
    col_index = lax.axis_index("pcol")
    block_rows = anc_inverse.shape[0]
    block_cols = anc_inverse.shape[1]
    steps_total = pivot_inverse.shape[0]
    width = pivot_inverse.shape[1]
    all_cols = anc_factor.shape[1]
    block_count = structure.shape[1]
    ratio_cols = col_count // row_count
    share_rows = block_rows // col_count
    structure_cols = structure.T.astype(jnp.float32)
    global_rows = col_index * block_cols + lax.iota(jnp.int32, block_cols)
    onehot_rows = (
        (global_rows // width)[:, None] == lax.iota(jnp.int32, block_count)[None, :]
    ).astype(jnp.float32)
    kept_rows = product(onehot_rows, structure_cols)
    share_offset = col_index * share_rows
    share_global = (row_index * col_count + col_index) * share_rows + lax.iota(
        jnp.int32, share_rows
    )
    onehot_share = (
        (share_global // width)[:, None] == lax.iota(jnp.int32, block_count)[None, :]
    ).astype(jnp.float32)
    kept_share = product(onehot_share, structure_cols)
    slot_ids = lax.iota(jnp.int32, col_count)
    source_flag = (slot_ids // row_count == col_index - row_index * ratio_cols).astype(jnp.float32)
    pieces = jnp.tile(anc_factor.reshape(row_count, share_rows, all_cols), (ratio_cols, 1, 1))
    outgoing = pieces * source_flag[:, None, None]
    incoming = lax.all_to_all(outgoing, "pcol", split_axis=0, concat_axis=0, tiled=True)
    factor_share = jnp.sum(incoming, axis=0)
    column_store = {}
    share_store = {}
    window_blocks = {}
    for k in range(steps_total - 1, -1, -1):
        first_col = k * width
        factor_now = anc_factor[:, first_col : first_col + width] * kept_rows[:, k : k + 1]
        share_factor = factor_share[:, first_col : first_col + width] * kept_share[:, k : k + 1]
        finished = list(range(k + 1, steps_total))
        if finished:
            stacked = jnp.concatenate([column_store[j] for j in finished], axis=1)
            factor_win = win_factor[first_col + width :, first_col : first_col + width]

        def term_rows(start, count, factor_now=factor_now):
            return product(anc_inverse, factor_now)

        share_image = lax.psum_scatter(
            term_rows(jnp.int32(0), share_rows * lax.axis_size("pcol")),
            "pcol",
            scatter_dimension=0,
            tiled=True,
        )
        if finished:
            share_image = share_image + product(
                lax.dynamic_slice_in_dim(stacked, share_offset, share_rows, 0), factor_win
            )
        share_column = -share_image
        column_now = lax.all_gather(share_column, "pcol", axis=0, tiled=True)
        crossings = [product(share_store[j].T, share_factor) for j in finished]
        pivot_part = product(share_factor.T, share_column)
        cross_sums = []
        if finished:
            cross_total = lax.psum(jnp.stack(crossings), ("prow", "pcol"))
            cross_sums = [cross_total[position] for position in range(len(finished))]
        pivot_sum = lax.psum(pivot_part, ("prow", "pcol"))
        for position, j in enumerate(finished):
            running = cross_sums[position]
            for i in finished:
                running = running + product(
                    window_blocks[j, i],
                    win_factor[i * width : (i + 1) * width, first_col : first_col + width],
                )
            window_blocks[j, k] = -running
            window_blocks[k, j] = -running.T
        pivot_block = pivot_inverse[k] - pivot_sum
        for j in finished:
            pivot_block = pivot_block - product(
                win_factor[j * width : (j + 1) * width, first_col : first_col + width].T,
                window_blocks[j, k],
            )
        window_blocks[k, k] = pivot_block
        column_store[k] = column_now
        share_store[k] = share_column
    anc_columns = jnp.concatenate([share_store[k] for k in range(steps_total)], axis=1)
    win_inverse = jnp.concatenate(
        [
            jnp.concatenate([window_blocks[i, k] for k in range(steps_total)], axis=1)
            for i in range(steps_total)
        ],
        axis=0,
    )
    return (anc_columns, win_inverse)


vmem_bytes = 56 * 1024 * 1024
tile = 128
little = pl.CostEstimate(flops=1, bytes_accessed=1, transcendentals=0)


def halves_of(value):
    high = value.astype(jnp.bfloat16)
    return high, (value - high.astype(jnp.float32)).astype(jnp.bfloat16)


def product_of(left, right, turned=False):
    dims = ((0,), (0,)) if turned else ((1,), (0,))

    def dot(a, b):
        return lax.dot_general(a, b, (dims, ((), ())), preferred_element_type=jnp.float32)

    return dot(left[0], right[0]) + dot(left[0], right[1]) + dot(left[1], right[0])


def times(left, right, turned=False):
    return product_of(halves_of(left), halves_of(right), turned)


def chip_at(place, levels):
    return jnp.where(place < levels, 2 * place, 2 * (2 * levels - 1 - place) + 1)


def ring_place(index, levels):
    z = index // 4
    return jnp.where((index // 2) % 2 == 0, z, 2 * levels - 1 - z)


def source_device(step, index, levels):
    away = jnp.where(step % 2 == 1, -((step + 1) // 2), step // 2)
    spot = lax.rem(ring_place(index, levels) + away + 2 * levels, 2 * levels)
    return 2 * chip_at(spot, levels) + index % 2


def head_kernel(width, cuts, index_ref, structure_ref, factor_ref, masked_ref, *turned_refs):
    rows, all_cols = factor_ref.shape
    share = math.gcd(rows, width)
    for t in range(rows // share):
        block = (index_ref[0] * rows + t * share) // width
        at = slice(t * share, (t + 1) * share)
        for k in range(all_cols // width):
            kept = structure_ref[k, block].astype(jnp.float32)
            cols = slice(k * width, (k + 1) * width)
            masked_ref[at, cols] = factor_ref[at, cols] * kept
    for (first, last), ref in zip(cuts, turned_refs):
        ref[...] = masked_ref[:, first:last].T


def head(index, structure, anc_factor, width, cuts):
    rows, all_cols = anc_factor.shape
    smem = pl.BlockSpec(memory_space=pltpu.SMEM)
    vmem = pl.BlockSpec(memory_space=pltpu.VMEM)
    return pl.pallas_call(
        functools.partial(head_kernel, width, cuts),
        in_specs=[smem, smem, vmem],
        out_specs=[vmem] * (1 + len(cuts)),
        out_shape=[jax.ShapeDtypeStruct((rows, all_cols), jnp.float32)]
        + [jax.ShapeDtypeStruct((last - first, rows), jnp.float32) for first, last in cuts],
        compiler_params=pltpu.CompilerParams(vmem_limit_bytes=vmem_bytes),
        cost_estimate=little,
    )(index, structure, anc_factor)


def multiply_kernel(layout, has_start, rows_at, index_ref, *refs):
    refs = list(refs)
    late = []
    if rows_at:
        sem = refs.pop()
        kept = [refs.pop() for _ in range(4)][::-1]
    sources = [refs.pop(0) for _ in range(4)]
    piece_count = sum(len(block) for block in layout)
    pieces = [refs.pop(0) for _ in range(piece_count)]
    starts = [refs.pop(0) for _ in range(2)] if has_start else None
    factors = [refs.pop(0) for _ in range(2)] if rows_at else None
    outs = [refs.pop(0) for _ in range(2)]
    inner_ref = refs.pop(0) if rows_at else None
    held = refs.pop(0)
    rows = sources[0].shape[1]
    step = pl.program_id(0)
    if rows_at:
        last = rows_at[-1][1] + tile
        away = starts + [ref.at[:, pl.ds(0, last)] for ref in factors]
        late = [
            pltpu.make_async_copy(ref, place, sem.at[i])
            for i, (ref, place) in enumerate(zip(away, kept))
        ]
        for copy in late:
            copy.start()
        starts, factors = kept[:2], kept[2:]
    at = 0
    for b, block in enumerate(layout):
        chosen = pieces[at : at + len(block)]
        at += len(block)
        left = (b % 2) * rows

        @pl.when(step == b // 2)
        def _(chosen=chosen, block=block, left=left):
            for ref, (top, height) in zip(chosen, block):
                held[top : top + height, left : left + rows] = ref[...]

    if not rows_at:

        @pl.when(step == 0)
        def _():
            for i in range(2):
                outs[i][...] = starts[i][...] if has_start else jnp.zeros_like(outs[i])

    inverse = jnp.concatenate(
        [
            jnp.concatenate([own[...], twin[...]], axis=1)
            for own, twin in (sources[:2], sources[2:])
        ],
        axis=0,
    )
    value = product_of(halves_of(held[...]), halves_of(inverse))
    for copy in late[:2]:
        copy.wait()
    for i in range(2):
        before = starts[i] if rows_at else outs[i]
        outs[i][...] = before[...] + value[:, i * rows : (i + 1) * rows]
    for copy in late[2:]:
        copy.wait()
    if rows_at:

        @pl.when(step == len(layout) // 2 - 1)
        def _():
            image = halves_of(jnp.concatenate([out[...] for out in outs], axis=1))
            side = halves_of(jnp.concatenate([ref[...] for ref in factors], axis=0))
            spot = 0
            for start in range(0, len(rows_at), 2):
                group = rows_at[start : start + 2]
                top, last = group[0][0], group[-1][1] + tile
                value = product_of(
                    tuple(half[top : top + len(group) * tile] for half in image),
                    tuple(half[:, :last] for half in side),
                )
                for place, (_, first) in enumerate(group):
                    for i in range(first // tile + 1):
                        inner_ref[spot * tile : (spot + 1) * tile, :] = value[
                            place * tile : (place + 1) * tile, i * tile : (i + 1) * tile
                        ]
                        spot += 1


def multiply(index, inverse, twin, first, blocks, start=None, rows_at=(), factors=()):
    rows = inverse.shape[1]
    levels = inverse.shape[0] // rows // 4
    layout, flat = [], []
    for block in blocks:
        top, places = 0, []
        for piece in block:
            places.append((top, piece.shape[0]))
            top += piece.shape[0]
            flat.append(piece)
        layout.append(tuple(places))
    height = top

    def whole(shape):
        return pl.BlockSpec(shape, lambda i, at: (0, 0))

    def source(side):
        return pl.BlockSpec(
            (rows, rows), lambda i, at: (source_device(first + 2 * i + side, at[0], levels), 0)
        )

    image = jax.ShapeDtypeStruct((height, rows), jnp.float32)
    out_shape = [image, image]
    if rows_at:
        count = sum(first // tile + 1 for _, first in rows_at)
        out_shape.append(jax.ShapeDtypeStruct((count * tile, tile), jnp.float32))
    operands = flat + list(start or ()) + list(factors)
    scratch = []
    if rows_at:
        shapes = [(height, rows)] * 2 + [(rows, rows_at[-1][1] + tile)] * 2
        scratch = [pltpu.VMEM(shape, jnp.float32) for shape in shapes]
        scratch.append(pltpu.SemaphoreType.DMA((4,)))
    return pl.pallas_call(
        functools.partial(multiply_kernel, tuple(layout), start is not None, rows_at),
        grid_spec=pltpu.PrefetchScalarGridSpec(
            num_scalar_prefetch=1,
            grid=(len(blocks) // 2,),
            in_specs=[source(0), source(0), source(1), source(1)]
            + [whole(v.shape) for v in flat]
            + [pl.BlockSpec(memory_space=pl.ANY) if rows_at else whole(v.shape) for v in start or ()]
            + [pl.BlockSpec(memory_space=pl.ANY) for _ in factors],
            out_specs=[whole(v.shape) for v in out_shape],
            scratch_shapes=[pltpu.VMEM((height, 2 * rows), jnp.float32)] + scratch,
        ),
        out_shape=out_shape,
        compiler_params=pltpu.CompilerParams(vmem_limit_bytes=vmem_bytes),
        cost_estimate=little,
    )(index, inverse, twin, inverse, twin, *operands)


def columns_kernel(width, steps, image_ref, add_ref, factor_ref, out_ref):
    solved = {}
    for k in range(steps - 1, -1, -1):
        if k:
            at = slice((k - 1) * width, k * width)
            value = image_ref[at, :] + add_ref[at, :]
        else:
            value = jnp.zeros((width, image_ref.shape[1]), jnp.float32)
        for j in range(k + 1, steps):
            side = factor_ref[j * width : (j + 1) * width, k * width : (k + 1) * width]
            value = value + times(side, solved[j], True)
        solved[k] = -value
        out_ref[:, k * width : (k + 1) * width] = solved[k].T


def solve_columns(width, steps, image, add, win_factor):
    rows = image.shape[1]
    return pl.pallas_call(
        functools.partial(columns_kernel, width, steps),
        out_shape=jax.ShapeDtypeStruct((rows, steps * width), jnp.float32),
        compiler_params=pltpu.CompilerParams(vmem_limit_bytes=vmem_bytes),
        cost_estimate=little,
    )(image, add, win_factor)


def fill_inner(inner, top, one, two, first_half):
    whole = jnp.concatenate(
        [jnp.where(first_half, one, two), jnp.where(first_half, two, one)], axis=0
    )
    spot, row = 0, top
    while spot * tile < whole.shape[0]:
        for i in range(row // tile + 1):
            block = whole[spot * tile : (spot + 1) * tile]
            spot += 1
            inner[row : row + tile, i * tile : (i + 1) * tile] = block
            if i * tile < row:
                inner[i * tile : (i + 1) * tile, row : row + tile] = block.T
        row += tile


def last_kernel(
    core_ref, mine_ref, other_ref, image_ref, add_ref, columns_ref, base_ref, *refs
):
    columns_out, window_out, inner = refs
    columns_out[...] = columns_ref[...] - (image_ref[...] + add_ref[...]).T
    fill_inner(inner, 0, mine_ref[...], other_ref[...], core_ref[0] % 2 == 0)
    window_out[...] = base_ref[...] + inner[...]


def add_last(index, mine, other, image, add, columns, base):
    width, rows = image.shape
    column_block = pl.BlockSpec((rows, width), lambda i: (0, 0))
    window_block = pl.BlockSpec((width, width), lambda i: (0, 0))
    part = pl.BlockSpec(mine.shape, lambda i: (0, 0))
    whole = pl.BlockSpec(image.shape, lambda i: (0, 0))
    return pl.pallas_call(
        last_kernel,
        grid=(1,),
        in_specs=[pl.BlockSpec(memory_space=pltpu.SMEM), part, part, whole, whole]
        + [column_block, window_block],
        out_specs=[column_block, window_block],
        out_shape=[
            jax.ShapeDtypeStruct(columns.shape, jnp.float32),
            jax.ShapeDtypeStruct(base.shape, jnp.float32),
        ],
        input_output_aliases={5: 0, 6: 1},
        scratch_shapes=[pltpu.VMEM((width, width), jnp.float32)],
        compiler_params=pltpu.CompilerParams(vmem_limit_bytes=vmem_bytes),
        cost_estimate=little,
    )(index, mine, other, image, add, columns, base)


def window_kernel(width, steps, tops, core_ref, *refs):
    mine, other = refs[: len(tops)], refs[len(tops) : 2 * len(tops)]
    factor_ref, pivot_ref, out_ref, inner = refs[2 * len(tops) :]
    low = min(tops)
    if low:
        inner[:low, :low] = jnp.zeros((low, low), jnp.float32)
    for top, mine_ref, other_ref in zip(tops, mine, other):
        fill_inner(inner, top, mine_ref[...], other_ref[...], core_ref[0] % 2 == 0)

    def at(k):
        return slice(k * width, (k + 1) * width)

    cross = {}
    for k in range(steps - 1, -1, -1):
        later = range(k + 1, steps)
        for i in range(k + 1):
            value = inner[at(k), at(i)]
            for j in later:
                value = value + times(factor_ref[at(j), at(k)], cross[j, i], True)
            cross[k, i] = -value
        for j in later:
            value = cross[j, k]
            for i in later:
                value = value + times(out_ref[at(j), at(i)], factor_ref[at(i), at(k)])
            out_ref[at(j), at(k)] = -value
            out_ref[at(k), at(j)] = -value.T
        value = pivot_ref[k] - cross[k, k].T
        for j in later:
            value = value - times(factor_ref[at(j), at(k)], out_ref[at(j), at(k)], True)
        out_ref[at(k), at(k)] = value


def window_blocks_of(width, steps, tops, index, mine, other, win_factor, pivot_inverse):
    order = steps * width
    vmem = pl.BlockSpec(memory_space=pltpu.VMEM)
    count = 2 * len(tops) + 2
    return pl.pallas_call(
        functools.partial(window_kernel, width, steps, tops),
        in_specs=[pl.BlockSpec(memory_space=pltpu.SMEM)] + [vmem] * count,
        out_specs=vmem,
        out_shape=jax.ShapeDtypeStruct((order, order), jnp.float32),
        scratch_shapes=[pltpu.VMEM((order, order), jnp.float32)],
        compiler_params=pltpu.CompilerParams(vmem_limit_bytes=vmem_bytes),
        cost_estimate=little,
    )(index, *mine, *other, win_factor, pivot_inverse)


def fast(anc_inverse, anc_factor, win_factor, pivot_inverse, structure):
    n = lax.axis_size("pcol")
    index = lax.axis_index("pcol")
    levels = n // 4
    chips = n // 2
    half_way = chips // 2
    core = index % 2
    x = (index // 2) % 2
    z = index // 4
    rows = anc_inverse.shape[1]
    steps_total, width = pivot_inverse.shape[:2]
    all_cols = anc_factor.shape[1]
    order = [2 * s if s < levels else 2 * (chips - 1 - s) + 1 for s in range(chips)]
    forward = [
        (2 * order[s] + c, 2 * order[(s + 1) % chips] + c) for s in range(chips) for c in range(2)
    ]
    backward = [(to, start) for start, to in forward]

    def flip(bits):
        return [(p, p ^ bits) for p in range(n)]

    def send(value, pairs):
        return lax.ppermute(value, "pcol", pairs)

    def pick(value, at):
        return lax.dynamic_index_in_dim(value, at, 0, keepdims=False)

    def swap_halves(value, bit):
        halves = value.reshape((2, value.shape[0] // 2) + value.shape[1:])
        return pick(halves, bit), pick(halves, 1 - bit)

    def join(bit, mine, other):
        return jnp.concatenate(
            [jnp.where(bit == 0, mine, other), jnp.where(bit == 0, other, mine)], axis=0
        )

    def sum_small(value):
        mine, other = swap_halves(value, core)
        got = yield [send(other, flip(1))]
        mine = mine + got[0]
        got = yield [send(mine, flip(2))]
        mine = mine + got[0]
        got = yield [send(mine, flip(4 * d)) for d in range(1, levels)]
        for value in got:
            mine = mine + value
        got = yield [send(mine, flip(1))]
        yield mine, got[0]

    def sum_large(value):
        mine, other = swap_halves(value, core)
        got = yield [send(other, flip(1))]
        mine, other = swap_halves(mine + got[0], x)
        got = yield [send(other, flip(2))]
        mine = mine + got[0]
        parts = mine.reshape((levels, mine.shape[0] // levels) + mine.shape[1:])
        got = yield [send(pick(parts, z ^ d), flip(4 * d)) for d in range(1, levels)]
        total = pick(parts, z)
        for value in got:
            total = total + value
        got = yield [send(total, flip(4 * d)) for d in range(1, levels)]
        pieces = [total] + got
        bit = 1
        while bit < levels:
            pieces = [
                join((z // bit) % 2, pieces[i], pieces[i + 1]) for i in range(0, len(pieces), 2)
            ]
            bit *= 2
        mine = pieces[0]
        got = yield [send(mine, flip(2))]
        mine = join(x, mine, got[0])
        got = yield [send(mine, flip(1))]
        yield mine, got[0]

    def ends(up, down):
        middle = up.shape[0] // 2
        return [send(up[:middle], forward), send(down[middle:], backward)]

    at = index.astype(jnp.int32).reshape(1)
    plan = (((width, 2 * width), (2 * width, all_cols)), ((0, width),))
    cuts = tuple(cut for streams in plan for cut in streams)
    factor, *turned = head(at, structure, anc_factor, width, cuts)
    twin = send(anc_inverse, flip(1))
    factor_twin = send(factor, flip(1))
    factors = (factor, factor_twin)

    def ring(pieces):
        ups = downs = list(pieces)
        yield ups, ups
        for s in range(1, half_way):
            ups = [send(v, forward) for v in ups]
            downs = [send(v, backward) for v in downs]
            ups, downs = yield ups, downs
        if len(ups) == 2:
            yield [send(ups[0], forward), send(downs[1], backward)]
        else:
            yield ends(ups[0], downs[0])

    def strips(streams):
        first, last = streams[0][0], streams[-1][1]
        return tuple((i - first, i) for i in range(first, last, tile))

    def product(start, blocks, total=None, rows_at=()):
        return multiply(
            at, anc_inverse, twin, start, blocks, total, rows_at, factors if rows_at else ()
        )

    hold = lax.optimization_barrier
    ring_a = ring(turned[: len(plan[0])])
    pieces_b = turned[len(plan[0]) :]
    a = [next(ring_a)[0]]
    ups_a, downs_a = next(ring_a)
    a += [ups_a, downs_a]
    ups_a, downs_a = ring_a.send((ups_a, downs_a))
    a += [ups_a, downs_a]
    ups_a, downs_a = ring_a.send((ups_a, downs_a))
    near = product(0, a[:4])
    (ups_a, downs_a), near = hold(((ups_a, downs_a), near))
    pieces_b, downs_a = hold((pieces_b, downs_a))
    far = ring_a.send((ups_a, downs_a))
    a += [ups_a, downs_a, far]
    ring_b = ring(pieces_b)
    b = [next(ring_b)[0]]
    ups_b, downs_b = next(ring_b)
    mid = product(4, a[4:6], near)
    mine_a, theirs_a, local = product(6, a[6:], mid, strips(plan[0]))
    (ups_b, downs_b), local = hold(((ups_b, downs_b), local))
    sum_a = sum_large(local)
    got = next(sum_a)
    got = sum_a.send(got)
    b += [ups_b, downs_b]
    ups_b, downs_b = ring_b.send((ups_b, downs_b))
    adds_a = send(theirs_a, flip(1))
    b += [ups_b, downs_b]
    near = product(0, b[:4])
    (ups_b, downs_b), got, near = hold(((ups_b, downs_b), got, near))
    got = sum_a.send(got)
    ups_b, downs_b = ring_b.send((ups_b, downs_b))
    b += [ups_b, downs_b]
    mid = product(4, b[4:6], near)
    columns = solve_columns(width, steps_total, mine_a, adds_a, win_factor)
    got, mid, columns = hold((got, mid, columns))
    got = sum_a.send(got)
    b += [ring_b.send((ups_b, downs_b))]
    mine_b, theirs_b, local = product(6, b[6:], mid, strips(plan[1]))
    adds_b = send(theirs_b, flip(1))
    sum_b = sum_small(local)
    got_b = next(sum_b)
    got = sum_a.send(got)
    got_b, got = hold((got_b, got))
    got_b = sum_b.send(got_b)
    got = sum_a.send(got)
    got_b, got = hold((got_b, got))
    got_b = sum_b.send(got_b)
    mine, other = sum_a.send(got)
    base = window_blocks_of(
        width, steps_total, (width,), at, [mine], [other], win_factor, pivot_inverse
    )
    got_b, base = hold((got_b, base))
    got_b = sum_b.send(got_b)
    anc_columns, win_inverse = add_last(
        at, *sum_b.send(got_b), mine_b, adds_b, columns, base
    )
    return (anc_columns, win_inverse)


def solution(mesh):
    in_specs = (
        P(("pole", "prow"), "pcol"),
        P(("pole", "pcol"), None),
        P("pole", None),
        P("pole", None, None),
        P(),
    )
    out_specs = (P(("pole", "prow", "pcol"), None), P("pole", None))
    ringed = mesh.shape["prow"] == 1 and mesh.shape["pcol"] == 16
    return jax.shard_map(
        fast if ringed else on_device, mesh=mesh, in_specs=in_specs, out_specs=out_specs, check_vma=False
    )
```
